128 devices in a mesh: row: 8 (over z_hi, y), col: 16 (over x, z_lo, core).
Axes of the slice: x: 4, y: 4, z: 4 (z_hi: 2, z_lo: 2; z = z_hi * 2 + z_lo), core: 2. Of those that a mesh axis runs over, the one named last changes fastest.
Arguments:
- cooc: int32 [16384, 32768], P('row', 'col'), may hold values from 0 to 48
- tile_list: int32 [8, 16, 4], P('row', 'col'), may hold values from -1 to 3, as said below
- marginal: int32 [32768], P(('col', 'row')), may hold values from 8 to 524287
- embed: float32 [32768, 256], P(('col', 'row')), may hold values from -1.5 to 1.5
- accum: float32 [32768, 256], P(('col', 'row')), may hold values from 0.001 to 0.01
Outputs:
- new_embed: float32 [32768, 256], P(('col', 'row'))
- new_accum: float32 [32768, 256], P(('col', 'row'))
The draws below stay inside these ranges and needn't reach their ends.
Inputs may be any that keep to these rules, and one draw needn't show every extreme that they name: `tile_list`: the first entries of each device's list are distinct local tile numbers, the rest are -1; every device lists at least one tile and some device lists all 4.
All inputs are finite; a program needn't handle non-finite values.
Results may differ from the reference program's by a relative error of at most 0.0003.
Values sent between devices are 32-bit elements; how exact they have to be, the bound alone decides.
A program may use at most 128 MiB of HBM per device.

```python
import math
import jax
import jax.numpy as jnp
from jax import lax

D = 256
BLOCK = 1024
RB = 2
CB = 2
ROWGROUPS = 8
COLGROUPS = 16
TILES_DEV = 4
SLAB_ROWS = 16384
VOCAB = 32768


def draw_cooc(key, part):
    key = jax.random.fold_in(key, 11)
    drawn = jax.random.randint(key, (SLAB_ROWS, VOCAB), 0, 96, dtype=jnp.int32)
    return jnp.maximum(drawn - 47, 0).astype(jnp.int32)


def draw_tile_list(key, part):
    key = jax.random.fold_in(key, 5)
    first, second, third, fourth = jax.random.split(key, 4)
    devices = ROWGROUPS * COLGROUPS
    scores_int = jax.random.randint(first, (devices, TILES_DEV), 0, 1 << 20, dtype=jnp.int32) * TILES_DEV + jnp.arange(TILES_DEV, dtype=jnp.int32)[None, :]
    ordering = jnp.argsort(scores_int, axis=1, stable=True).astype(jnp.int32)
    light = jax.random.randint(second, (devices,), 0, 8, dtype=jnp.int32) < 5
    listed = jnp.where(light, 1, jax.random.randint(third, (devices,), 1, TILES_DEV + 1, dtype=jnp.int32))
    fullest = jax.random.randint(fourth, (), 0, devices, dtype=jnp.int32)
    listed = jnp.where(jnp.arange(devices, dtype=jnp.int32) == fullest, TILES_DEV, listed)
    position = jnp.arange(TILES_DEV, dtype=jnp.int32)[None, :]
    chosen = jnp.where(position < listed[:, None], ordering, -1)
    return chosen.reshape(ROWGROUPS, COLGROUPS, TILES_DEV).astype(jnp.int32)


def draw_marginal(key, part):
    key = jax.random.fold_in(key, 7)
    first, second, third, fourth = jax.random.split(key, 4)
    items = jnp.arange(VOCAB, dtype=jnp.int32)
    exponent = jax.random.randint(first, (VOCAB,), 3, 18, dtype=jnp.int32) + 2 * items // VOCAB
    lowest = jnp.left_shift(jnp.ones((VOCAB,), jnp.int32), exponent)
    extra = jax.random.randint(second, (VOCAB,), 0, lowest, dtype=jnp.int32)
    values = lowest + extra
    low_item = jax.random.randint(third, (), 0, VOCAB, dtype=jnp.int32)
    high_item = (low_item + 1 + jax.random.randint(fourth, (), 0, VOCAB - 1, dtype=jnp.int32)) % VOCAB
    values = jnp.where(items == low_item, 8, values)
    values = jnp.where(items == high_item, 524287, values)
    return values.astype(jnp.int32)


def level_of(rng, dims, cuts, low, largest):
    def one(dim, shards_of):
        heights = jax.random.uniform(jax.random.fold_in(jax.random.fold_in(rng, 6), dim), (shards_of,), jnp.float32, low / len(cuts), largest / len(cuts))
        return jnp.repeat(jnp.exp(heights), dims[dim] // shards_of).reshape((-1,) + (1,) * (len(dims) - dim - 1))

    level = one(*cuts[0])
    for cut in cuts[1:]:
        level = level * one(*cut)
    return level


def bell_draw(own_key, dims, scale, reach, pieces=(), kind=jnp.bfloat16):
    values = jax.random.normal(own_key, dims, jnp.float32) * scale
    if len(pieces) > 0:
        values = level_of(own_key, dims, pieces, -0.22, 0.18) * values
    return jnp.clip(values, min=-reach, max=reach).astype(kind)


def setup_inputs(seed: int = 0) -> dict:
    key_of = jax.random.split(jax.random.key(seed), 6)
    return {
        "cooc": draw_cooc(jax.random.fold_in(key_of[5], 71), 0),
        "tile_list": draw_tile_list(jax.random.fold_in(key_of[5], 71), 0),
        "marginal": draw_marginal(jax.random.fold_in(key_of[5], 71), 0),
        "embed": bell_draw(key_of[3], (VOCAB, D), 0.25, 1.5, ((0, 128),), jnp.float32),
        "accum": jnp.clip(jnp.exp(math.log(0.01) - 2.30258502 * jax.random.uniform(key_of[4], (VOCAB, D), jnp.float32) ** level_of(key_of[4], (VOCAB, D), ((0, 128),), -0.2, 0.2)), 0.001, 0.01),
    }


LEARN_RATE = 0.05

def tile_grads(counts, row_vecs, col_vecs, row_logs, col_logs, log_total):
    scores = lax.dot_general(row_vecs, col_vecs, (((1,), (1,)), ((), ())), precision=lax.Precision.HIGHEST, preferred_element_type=jnp.float32)
    centred = scores + row_logs[:, None] + col_logs[None, :] - log_total
    counts_f = counts.astype(jnp.float32)
    weights = 0.1 + 0.25 * jnp.sqrt(counts_f)
    slopes = jnp.where(counts > 0, weights * (centred - jnp.log(jnp.maximum(counts_f, 1.0))), jax.nn.sigmoid(centred))
    to_rows = jnp.dot(slopes, col_vecs, precision=lax.Precision.HIGHEST, preferred_element_type=jnp.float32)
    to_cols = lax.dot_general(slopes, row_vecs, (((0,), (0,)), ((), ())), precision=lax.Precision.HIGHEST, preferred_element_type=jnp.float32)
    return (to_rows, to_cols)

def reference(cooc, tile_list, marginal, embed, accum):
    marg_f = marginal.astype(jnp.float32)
    log_marg = jnp.log(marg_f)
    log_total = jnp.log(jnp.sum(marg_f))
    flat_list = tile_list.reshape(-1)

    def visit(gradients, flat_index):
        entry = flat_list[flat_index]
        group = flat_index // TILES_DEV
        row_group = group // COLGROUPS
        col_group = group % COLGROUPS
        tile_local = jnp.maximum(entry, 0)
        row_start = ((row_group * RB + tile_local // CB) * BLOCK).astype(jnp.int32)
        col_start = ((col_group * CB + tile_local % CB) * BLOCK).astype(jnp.int32)

        def with_tile(current):
            counts = lax.dynamic_slice(cooc, (row_start, col_start), (BLOCK, BLOCK))
            row_vecs = lax.dynamic_slice_in_dim(embed, row_start, BLOCK, 0)
            col_vecs = lax.dynamic_slice_in_dim(embed, col_start, BLOCK, 0)
            row_logs = lax.dynamic_slice_in_dim(log_marg, row_start, BLOCK, 0)
            col_logs = lax.dynamic_slice_in_dim(log_marg, col_start, BLOCK, 0)
            to_rows, to_cols = tile_grads(counts, row_vecs, col_vecs, row_logs, col_logs, log_total)
            current = lax.dynamic_update_slice_in_dim(current, lax.dynamic_slice_in_dim(current, row_start, BLOCK, 0) + to_rows, row_start, 0)
            current = lax.dynamic_update_slice_in_dim(current, lax.dynamic_slice_in_dim(current, col_start, BLOCK, 0) + to_cols, col_start, 0)
            return current

        def unchanged(current):
            return current
        return (lax.cond(entry >= 0, with_tile, unchanged, gradients), None)
    start = jnp.zeros(embed.shape, jnp.float32)
    gradients, _ = lax.scan(visit, start, jnp.arange(ROWGROUPS * COLGROUPS * TILES_DEV, dtype=jnp.int32))
    gradients = gradients / BLOCK
    new_accum = accum + gradients * gradients
    new_embed = embed - LEARN_RATE * gradients / jnp.sqrt(new_accum)
    return (new_embed, new_accum)
```

```python
import functools

import jax
import jax.numpy as jnp
from jax import lax
from jax.experimental import pallas as pl
from jax.experimental.pallas import tpu as pltpu
from jax.sharding import PartitionSpec as P

LEARN_RATE = 0.05
MESH = pl.DeviceIdType.MESH
PAD = 8
RING = 4
N_SEND = 80
N_RECV = 64


def split(value):
    high = value.astype(jnp.bfloat16)
    low = (value - high.astype(jnp.float32)).astype(jnp.bfloat16)
    return high, low


class Copies:
    def __init__(self, send_sems, recv_sems):
        self.send_sems, self.recv_sems = send_sems, recv_sems
        self.sends = self.recvs = 0
        self.pending = []

    def send_sem(self):
        self.sends += 1
        return self.send_sems.at[self.sends - 1]

    def recv_sem(self, count=1):
        self.recvs += count
        return self.recvs - count

    def start(self, src, dst, device):
        copy = pltpu.make_async_remote_copy(
            src_ref=src,
            dst_ref=dst,
            send_sem=self.send_sem(),
            recv_sem=self.recv_sems.at[self.recv_sem()],
            device_id=device,
            device_id_type=MESH,
        )
        copy.start()
        self.pending.append(copy)
        return copy

    def finish(self):
        for copy in self.pending:
            copy.wait_send()


def kernel(
    block,
    embed_hbm,
    marg_ref,
    tiles_ref,
    accum_hbm,
    cooc_hbm,
    new_embed_ref,
    new_accum_ref,
    col_land,
    row_land,
    row_src,
    cooc_v,
    accum_v,
    e_hi,
    e_lo,
    et_hi,
    et_lo,
    c_hi,
    c_lo,
    row_log,
    col_log,
    row_grad,
    col_grad,
    sib_in,
    row_in1,
    row_in2,
    row_in3,
    row_in4,
    col_in1,
    col_in2,
    col_in3,
    tot1,
    tot2,
    tot3,
    send_sems,
    recv_sems,
    local_sems,
):
    share, width = embed_hbm.shape
    half = share // 2
    row = lax.axis_index("row")
    col = lax.axis_index("col")
    zh, y = row // 4, lax.rem(row, 4)
    x, zl, q = col // 4, lax.rem(col // 2, 2), lax.rem(col, 2)

    def device(zh_=zh, y_=y, x_=x, zl_=zl, q_=q):
        return (zh_ * 4 + y_, x_ * 4 + zl_ * 2 + q_)

    def ring(position, step):
        return lax.rem(position + step + RING, RING)

    x_up, x_down, x_far = ring(x, 1), ring(x, -1), ring(x, 2)
    y_up, y_down, y_far = ring(y, 1), ring(y, -1), ring(y, 2)
    is_owner = col < 8

    def flip(bit, by):
        return 1 - bit if by else bit

    near = [
        device(zh_=flip(zh, k // 4), zl_=flip(zl, k // 2 % 2), q_=flip(q, k % 2))
        for k in range(1, 8)
    ]
    near_y = [device(y_=ring(y, k)) for k in range(1, 4)]
    near_x = [device(x_=ring(x, k)) for k in range(1, 4)]
    sibling, zl_pair, zh_pair = near[0], near[1], near[3]
    source = (zl * 4 + ring(x, -1), row)
    targets = [(col, ring(y, 1) * 4 + zh * 2 + k) for k in range(2)]

    embed_in = pltpu.make_async_copy(
        embed_hbm, col_land.at[zh, y, pl.ds(0, share)], local_sems.at[0]
    )
    embed_in.start()
    accum_in = pltpu.make_async_copy(accum_hbm, accum_v, local_sems.at[1])
    accum_in.start()
    cooc_in = []
    for p in range(8):
        copy = pltpu.make_async_copy(
            cooc_hbm.at[pl.ds(p * share, share)],
            cooc_v.at[pl.ds(p * share, share)],
            local_sems.at[2 + p],
        )
        copy.start()
        cooc_in.append(copy)

    barrier = pltpu.get_barrier_semaphore()
    for other in near + near_y + near_x + [source]:
        pl.semaphore_signal(barrier, inc=1, device_id=other, device_id_type=MESH)

    @pl.when(is_owner)
    def _():
        for other in targets:
            pl.semaphore_signal(barrier, inc=1, device_id=other, device_id_type=MESH)

    marg = marg_ref[...].astype(jnp.float32)
    logs = jnp.log(marg)
    tot1[0] = jnp.broadcast_to(jnp.sum(marg, axis=1, keepdims=True), tot1.shape[1:])

    @pl.when(is_owner)
    def _():
        pl.semaphore_wait(barrier, 16)

    @pl.when(jnp.logical_not(is_owner))
    def _():
        pl.semaphore_wait(barrier, 14)

    net = Copies(send_sems, recv_sems)

    def spread(block_ref, others):
        sem = recv_sems.at[net.recv_sem()]
        count = len(others)
        for k, other in enumerate(others):
            copy = pltpu.make_async_remote_copy(
                src_ref=block_ref.at[0],
                dst_ref=block_ref.at[k + 1],
                send_sem=net.send_sem(),
                recv_sem=sem,
                device_id=other,
                device_id_type=MESH,
            )
            copy.start()
            net.pending.append(copy)
        landed = block_ref.at[pl.ds(1, count)]
        return pltpu.make_async_copy(landed, landed, sem)

    stage1 = spread(tot1, near)

    embed_in.wait()
    col_land[zh, y, pl.ds(share, PAD), :] = jnp.broadcast_to(logs, (PAD, width))
    for h in range(2):
        row_src[h, pl.ds(0, half), :] = col_land[zh, y, pl.ds(h * half, half), :]
        row_src[h, pl.ds(half, PAD), :] = jnp.broadcast_to(
            jnp.concatenate([logs[:, h * half : (h + 1) * half]] * 2, axis=1), (PAD, width)
        )
    scatter_recv = recv_sems.at[net.recv_sem()]
    scatter = [
        pltpu.make_async_remote_copy(
            src_ref=row_src.at[k],
            dst_ref=row_land.at[zh, y_up, k],
            send_sem=net.send_sem(),
            recv_sem=scatter_recv,
            device_id=targets[k],
            device_id_type=MESH,
        )
        for k in range(2)
    ]

    @pl.when(is_owner)
    def _():
        for copy in scatter:
            copy.start()

    def whole(land, index):
        return land.at[index]

    def first(land, index):
        return land.at[(*index, pl.ds(0, land.shape[-2] // 16 * 8 + PAD))]

    def second(land, index):
        start = land.shape[-2] // 16 * 8 + PAD
        return land.at[(*index, pl.ds(start, land.shape[-2] - start))]

    def send(view, land, index, other):
        part = view(land, index)
        return net.start(part, part, other)

    c0, c1 = zh, 1 - zh
    near_pair = send(whole, col_land, (c0, y), zh_pair)
    col_up = send(whole, col_land, (c0, y), near_y[0])
    col_down = send(whole, col_land, (c0, y), near_y[2])

    stage1.wait()
    tot2[0] = jnp.sum(tot1[...], axis=0)
    stage2 = spread(tot2, near_y)

    r0, r1 = zl, 1 - zl
    scatter[0].wait_recv()
    row_pair = send(whole, row_land, (r0, x, q), zl_pair)
    row_up = send(whole, row_land, (r0, x, q), near_x[0])
    row_down = send(whole, row_land, (r0, x, q), near_x[2])
    sib = [send(whole, row_land, (r0, x, q), sibling)]

    stage2.wait()
    tot3[0] = jnp.sum(tot2[...], axis=0)
    stage3 = spread(tot3, near_x)

    col_up.wait_recv()
    col_far_up = send(first, col_land, (c0, y_down), near_y[0])
    col_down.wait_recv()
    col_far_down = send(second, col_land, (c0, y_up), near_y[2])

    row_up.wait_recv()
    row_far_up = send(first, row_land, (r0, x_down, q), near_x[0])
    sib.append(send(whole, row_land, (r0, x_down, q), sibling))
    row_down.wait_recv()
    row_far_down = send(second, row_land, (r0, x_up, q), near_x[2])
    sib.append(send(whole, row_land, (r0, x_up, q), sibling))

    row_pair.wait_recv()
    row_up = send(whole, row_land, (r1, x, q), near_x[0])
    row_down = send(whole, row_land, (r1, x, q), near_x[2])
    sib.append(send(whole, row_land, (r1, x, q), sibling))

    near_pair.wait_recv()
    col_up = send(whole, col_land, (c1, y), near_y[0])
    col_down = send(whole, col_land, (c1, y), near_y[2])

    stage3.wait()
    log_total = jnp.log(jnp.sum(tot3[...], axis=0))[:1, :1]

    row_far_up.wait_recv()
    row_far_down.wait_recv()
    sib.append(send(whole, row_land, (r0, x_far, q), sibling))
    row_up.wait_recv()
    row_far_up = send(first, row_land, (r1, x_down, q), near_x[0])
    sib.append(send(whole, row_land, (r1, x_down, q), sibling))
    row_down.wait_recv()
    row_far_down = send(second, row_land, (r1, x_up, q), near_x[2])
    sib.append(send(whole, row_land, (r1, x_up, q), sibling))

    col_far_up.wait_recv()
    col_far_down.wait_recv()
    col_up.wait_recv()
    col_far_up = send(first, col_land, (c1, y_down), near_y[0])
    col_down.wait_recv()
    col_far_down = send(second, col_land, (c1, y_up), near_y[2])

    row_far_up.wait_recv()
    row_far_down.wait_recv()
    sib.append(send(whole, row_land, (r1, x_far, q), sibling))
    for copy in sib:
        copy.wait_recv()
    col_far_up.wait_recv()
    col_far_down.wait_recv()

    def convert(p, carry):
        g, w = p // 4, lax.rem(p, 4)
        rows = pl.ds(pl.multiple_of(p * share, share), share)
        c_hi[rows, :], c_lo[rows, :] = split(col_land[g, w, pl.ds(0, share), :])
        col_log[p] = col_land[g, w, pl.ds(share, PAD), :] - log_total
        at = ring(w, 1)
        piece = jnp.concatenate(
            [row_land[g, at, 0, pl.ds(0, half), :], row_land[g, at, 1, pl.ds(0, half), :]], axis=0
        )
        e_hi[rows, :], e_lo[rows, :] = split(piece)
        flipped = piece.T
        et_hi[p], et_lo[p] = split(flipped)
        for h in range(2):
            line = row_land[g, at, h, pl.ds(half, 1), pl.ds(0, half)]
            row_log[pl.ds(pl.multiple_of(p * share + h * half, half), half), :] = jnp.broadcast_to(
                line, (128, half)
            ).T
        return carry

    lax.fori_loop(0, 8, convert, 0)

    row_grad[...] = jnp.zeros_like(row_grad)
    col_grad[...] = jnp.zeros_like(col_grad)
    for copy in cooc_in:
        copy.wait()

    entries = [tiles_ref[0, k] for k in range(4)]

    def listed(t):
        on = [jnp.where(entry == t, jnp.float32(1), jnp.float32(0)) for entry in entries]
        return (on[0] + on[1]) + (on[2] + on[3])

    def chunk(step, carry):
        p, j = step // 2, lax.rem(step, 2)
        on = listed(p // 4 * 2 + j)
        rows = pl.ds(pl.multiple_of(p * share, share), share)
        eh = e_hi[rows, :]
        rows_cat = jnp.concatenate([eh, eh, e_lo[rows, :]], axis=1)
        th = et_hi[p]
        flipped_cat = jnp.concatenate([th, et_lo[p], th], axis=1)
        logs_row = jnp.concatenate([row_log[rows, :]] * (share // 128), axis=1)
        to_rows = jnp.zeros((share, width), jnp.float32)
        for k in range(4):
            pc = j * 4 + k
            cols = pl.ds(pl.multiple_of(pc * share, share), share)
            ch, cl = c_hi[cols, :], c_lo[cols, :]
            scores = lax.dot_general(
                rows_cat,
                jnp.concatenate([ch, cl, ch], axis=1),
                (((1,), (1,)), ((), ())),
                preferred_element_type=jnp.float32,
            )
            centred = scores + logs_row + col_log[pc, :1, :]
            counts = cooc_v[rows, cols]
            counts_f = jnp.maximum(counts.astype(jnp.float32), 1.0)
            slopes = on * jnp.where(
                counts > 0,
                (0.1 + 0.25 * jnp.sqrt(counts_f)) * (centred - jnp.log(counts_f)),
                1.0 / (1.0 + jnp.exp(-centred)),
            )
            sh, sl = split(slopes)
            to_rows += jnp.dot(
                jnp.concatenate([sh, sh, sl], axis=1),
                jnp.concatenate([ch, cl, ch], axis=0),
                preferred_element_type=jnp.float32,
            )
            col_grad[j, k] += jnp.dot(
                flipped_cat,
                jnp.concatenate([sh, sh, sl], axis=0),
                preferred_element_type=jnp.float32,
            )
        at = ring(lax.rem(p, 4), 1)
        for h in range(2):
            row_grad[h, p // 4, at] += to_rows[h * half : (h + 1) * half]
        return carry

    lax.fori_loop(0, 16, chunk, 0)

    from_sib = net.start(row_grad.at[1 - q], sib_in, sibling)

    def col_part(index, upper):
        return col_grad.at[index[0], index[1], pl.ds(upper * (width // 2), width // 2)]

    def row_part(g, at, upper):
        return row_grad.at[q, g, at, pl.ds(upper * (half // 2), half // 2)]

    col_first = [
        (
            net.start(col_part((g, y_far), 0), col_in1.at[0, g], near_y[0]),
            net.start(col_part((g, y_far), 1), col_in1.at[1, g], near_y[2]),
        )
        for g in range(2)
    ]
    from_sib.wait_recv()
    row_grad[q] += sib_in[...]
    row_first = [
        (
            net.start(row_part(g, x_far, 0), row_in1.at[0, g], near_x[0]),
            net.start(row_part(g, x_far, 1), row_in1.at[1, g], near_x[2]),
        )
        for g in range(2)
    ]
    col_second, row_second = [], []
    for g in range(2):
        for copy in col_first[g]:
            copy.wait_recv()
        col_grad[g, y_up, pl.ds(0, width // 2), :] += col_in1[0, g]
        up = net.start(col_grad.at[g, y_up], col_in2.at[0, g], near_y[0])
        col_grad[g, y_down, pl.ds(width // 2, width // 2), :] += col_in1[1, g]
        down = net.start(col_grad.at[g, y_down], col_in2.at[1, g], near_y[2])
        col_second.append((up, down))
    for g in range(2):
        for copy in row_first[g]:
            copy.wait_recv()
        row_grad[q, g, x_up, pl.ds(0, half // 2), :] += row_in1[0, g]
        up = net.start(row_grad.at[q, g, x_up], row_in2.at[0, g], near_x[0])
        row_grad[q, g, x_down, pl.ds(half // 2, half // 2), :] += row_in1[1, g]
        down = net.start(row_grad.at[q, g, x_down], row_in2.at[1, g], near_x[2])
        row_second.append((up, down))
    for g in range(2):
        for copy in row_second[g]:
            copy.wait_recv()
        row_grad[q, g, x] += row_in2[0, g] + row_in2[1, g]
    row_last = net.start(row_grad.at[q, 1 - zl, x], row_in3, zl_pair)
    for g in range(2):
        for copy in col_second[g]:
            copy.wait_recv()
        col_grad[g, y] += col_in2[0, g] + col_in2[1, g]
    col_last = net.start(col_grad.at[1 - zh, y], col_in3, zh_pair)
    row_last.wait_recv()
    row_grad[q, zl, x] += row_in3[...]
    home_sem = net.recv_sem(2)
    home = pltpu.make_async_remote_copy(
        src_ref=row_grad.at[q, zl, x],
        dst_ref=row_in4.at[q],
        send_sem=net.send_sem(),
        recv_sem=recv_sems.at[home_sem + q],
        device_id=source,
        device_id_type=MESH,
    )
    home.start()
    net.pending.append(home)
    col_last.wait_recv()
    own = (col_grad[zh, y] + col_in3[...]).T
    accum_in.wait()

    def update(gradient):
        gradients = gradient * (1.0 / block)
        accum = accum_v[...] + gradients * gradients
        new_accum_ref[...] = accum
        new_embed_ref[...] = (
            col_land[zh, y, pl.ds(0, share), :] - LEARN_RATE * gradients / jnp.sqrt(accum)
        )

    @pl.when(is_owner)
    def _():
        for h in range(2):
            pltpu.make_async_copy(
                row_in4.at[h], row_in4.at[h], recv_sems.at[home_sem + h]
            ).wait()
        update(own + jnp.concatenate([row_in4[0], row_in4[1]], axis=0))
        for copy in scatter:
            copy.wait_send()

    @pl.when(jnp.logical_not(is_owner))
    def _():
        update(own)

    net.finish()


def local(cooc, tile_list, marginal, embed, accum):
    share, width = embed.shape
    half = share // 2
    items = 8 * share
    f32, bf16 = jnp.float32, jnp.bfloat16
    hbm = pl.BlockSpec(memory_space=pl.ANY)
    vmem = pl.BlockSpec(memory_space=pltpu.VMEM)
    smem = pl.BlockSpec(memory_space=pltpu.SMEM)
    shape = jax.ShapeDtypeStruct((share, width), f32)
    return pl.pallas_call(
        functools.partial(kernel, items // 2),
        out_shape=(shape, shape),
        in_specs=[hbm, vmem, smem, hbm, hbm],
        out_specs=(vmem, vmem),
        scratch_shapes=[
            pltpu.VMEM((2, 4, share + PAD, width), f32),
            pltpu.VMEM((2, 4, 2, half + PAD, width), f32),
            pltpu.VMEM((2, half + PAD, width), f32),
            pltpu.VMEM((items, items), jnp.int32),
            pltpu.VMEM((share, width), f32),
            pltpu.VMEM((items, width), bf16),
            pltpu.VMEM((items, width), bf16),
            pltpu.VMEM((8, width, share), bf16),
            pltpu.VMEM((8, width, share), bf16),
            pltpu.VMEM((items, width), bf16),
            pltpu.VMEM((items, width), bf16),
            pltpu.VMEM((items, 128), f32),
            pltpu.VMEM((8, PAD, share), f32),
            pltpu.VMEM((2, 2, 4, half, width), f32),
            pltpu.VMEM((2, 4, width, share), f32),
            pltpu.VMEM((2, 4, half, width), f32),
            pltpu.VMEM((2, 2, half // 2, width), f32),
            pltpu.VMEM((2, 2, half, width), f32),
            pltpu.VMEM((half, width), f32),
            pltpu.VMEM((2, half, width), f32),
            pltpu.VMEM((2, 2, width // 2, share), f32),
            pltpu.VMEM((2, 2, width, share), f32),
            pltpu.VMEM((width, share), f32),
            pltpu.VMEM((8, 8, 128), f32),
            pltpu.VMEM((4, 8, 128), f32),
            pltpu.VMEM((4, 8, 128), f32),
            pltpu.SemaphoreType.DMA((N_SEND,)),
            pltpu.SemaphoreType.DMA((N_RECV,)),
            pltpu.SemaphoreType.DMA((10,)),
        ],
        compiler_params=pltpu.CompilerParams(
            collective_id=0, has_side_effects=True, vmem_limit_bytes=56 * 2**20
        ),
        cost_estimate=pl.CostEstimate(
            flops=18 * items * items * width, bytes_accessed=4 * items * items, transcendentals=0
        ),
    )(embed, marginal.reshape(1, share), tile_list.reshape(1, 4), accum, cooc)


def solution(mesh):
    placed = (
        P("row", "col"),
        P("row", "col", None),
        P(("col", "row")),
        P(("col", "row"), None),
        P(("col", "row"), None),
    )
    return jax.shard_map(
        local,
        mesh=mesh,
        in_specs=placed,
        out_specs=(P(("col", "row"), None), P(("col", "row"), None)),
        check_vma=False,
    )
```

```python
import jax
import jax.numpy as jnp
from jax import lax
from jax.experimental import pallas as pl
from jax.experimental.pallas import tpu as pltpu
from jax.sharding import PartitionSpec as P

LEARN_RATE = 0.05
MESH = pl.DeviceIdType.MESH
PAD = 8
RING = 4
N_SEND = 64
N_RECV = 48


def split(value):
    high = value.astype(jnp.bfloat16)
    low = (value - high.astype(jnp.float32)).astype(jnp.bfloat16)
    return high, low


class Copies:
    def __init__(self, send_sems, recv_sems):
        self.send_sems, self.recv_sems = send_sems, recv_sems
        self.sends = self.recvs = 0
        self.pending = []

    def send_sem(self):
        self.sends += 1
        return self.send_sems.at[self.sends - 1]

    def recv_sem(self, count=1):
        self.recvs += count
        return self.recvs - count

    def make(self, src, dst, device):
        copy = pltpu.make_async_remote_copy(
            src_ref=src,
            dst_ref=dst,
            send_sem=self.send_sem(),
            recv_sem=self.recv_sems.at[self.recv_sem()],
            device_id=device,
            device_id_type=MESH,
        )
        self.pending.append(copy)
        return copy

    def finish(self):
        for copy in self.pending:
            copy.wait_send()


def kernel(
    embed_hbm,
    marg_ref,
    tiles_ref,
    cooc_hbm,
    grad_ref,
    col_land,
    row_land,
    row_src,
    cooc_v,
    e_hi,
    e_lo,
    et_hi,
    et_lo,
    c_hi,
    c_lo,
    row_log,
    col_log,
    scores_v,
    row_grad,
    col_grad,
    sib_in,
    row_in,
    row_home,
    col_in,
    col_last,
    tot1,
    tot2,
    tot3,
    send_sems,
    recv_sems,
    local_sems,
):
    share, width = embed_hbm.shape
    half = share // 2
    row = lax.axis_index("row")
    col = lax.axis_index("col")
    zh, y = row // 4, lax.rem(row, 4)
    x, zl, q = col // 4, lax.rem(col // 2, 2), lax.rem(col, 2)

    def device(zh_=zh, y_=y, x_=x, zl_=zl, q_=q):
        return (zh_ * 4 + y_, x_ * 4 + zl_ * 2 + q_)

    def ring(position, step):
        return lax.rem(position + step + RING, RING)

    def offset(o):
        return jnp.where(o == 0, 2, jnp.where(o == 1, 1, jnp.where(o == 2, 3, 0)))

    is_owner = col < 8

    def flip(bit, by):
        return 1 - bit if by else bit

    near = [
        device(zh_=flip(zh, k // 4), zl_=flip(zl, k // 2 % 2), q_=flip(q, k % 2))
        for k in range(1, 8)
    ]
    near_y = [device(y_=ring(y, k)) for k in range(1, 4)]
    near_x = [device(x_=ring(x, k)) for k in range(1, 4)]
    by_y = [near_y[1], near_y[0], near_y[2]]
    by_x = [near_x[1], near_x[0], near_x[2]]
    sibling, zl_pair, zh_pair = near[0], near[1], near[3]
    blocks = [lax.rem(zh + zl + s + y // 2, 2) for s in range(2)]

    def piece_y(x_):
        return lax.rem(zh + 1 + y - x_ + RING, RING)

    source = [(blocks[s] * 4 + piece_y(x), row) for s in range(2)]
    x_place = lax.rem(x + 1 - y + zl * 2 + q + RING, RING)
    zl_place = lax.rem(zl + zh + x, 2)
    targets = [
        [(col, x_place * 4 + lax.rem(zl_place + s, 2) * 2 + k) for k in range(2)] for s in range(2)
    ]

    embed_in = pltpu.make_async_copy(
        embed_hbm, col_land.at[zh, y, pl.ds(0, share)], local_sems.at[0]
    )
    embed_in.start()
    cooc_in = []
    for p in range(8):
        copy = pltpu.make_async_copy(
            cooc_hbm.at[pl.ds(p * share, share)],
            cooc_v.at[pl.ds(p * share, share)],
            local_sems.at[1 + p],
        )
        copy.start()
        cooc_in.append(copy)

    def signal(other):
        pl.semaphore_signal(barrier, inc=1, device_id=other, device_id_type=MESH)

    barrier = pltpu.get_barrier_semaphore()
    for other in near + near_y + near_x + [source[0]]:
        signal(other)

    @pl.when(is_owner)
    def _():
        for s in range(2):
            for other in targets[s]:
                signal(other)

    marg = marg_ref[...].astype(jnp.float32)
    logs = jnp.log(marg)
    tot1[0] = jnp.broadcast_to(jnp.sum(marg, axis=1, keepdims=True), tot1.shape[1:])
    embed_in.wait()
    col_land[zh, y, pl.ds(share, PAD), :] = jnp.broadcast_to(logs, (PAD, width))
    for h in range(2):
        row_src[h, pl.ds(0, half), :] = col_land[zh, y, pl.ds(h * half, half), :]
        row_src[h, pl.ds(half, PAD), :] = jnp.broadcast_to(
            jnp.concatenate([logs[:, h * half : (h + 1) * half]] * 2, axis=1), (PAD, width)
        )

    pl.semaphore_wait(barrier, 15 + jnp.where(is_owner, 2, 0))

    net = Copies(send_sems, recv_sems)

    def spread(block_ref, others):
        sem = recv_sems.at[net.recv_sem()]
        for k, other in enumerate(others):
            copy = pltpu.make_async_remote_copy(
                src_ref=block_ref.at[0],
                dst_ref=block_ref.at[k + 1],
                send_sem=net.send_sem(),
                recv_sem=sem,
                device_id=other,
                device_id_type=MESH,
            )
            copy.start()
            net.pending.append(copy)
        landed = block_ref.at[pl.ds(1, len(others))]
        return pltpu.make_async_copy(landed, landed, sem)

    def same(ref, other):
        return net.make(ref, ref, other)

    def start(copies):
        for copy in copies:
            copy.start()

    def arrive(copies):
        for copy in copies:
            copy.wait_recv()

    zls, zhs = (zl, 1 - zl), (zh, 1 - zh)
    scatter_recv = recv_sems.at[net.recv_sem()]
    scatter = [
        pltpu.make_async_remote_copy(
            src_ref=row_src.at[k],
            dst_ref=row_land.at[zl_place, k, x_place],
            send_sem=net.send_sem(),
            recv_sem=scatter_recv,
            device_id=targets[0][k],
            device_id_type=MESH,
        )
        for k in range(2)
    ]
    col_pair = same(col_land.at[zh, y], zh_pair)
    row_pair = same(row_land.at[zl, q, x], zl_pair)
    col_out = [[same(col_land.at[zhs[s], y], other) for other in by_y] for s in range(2)]
    row_out = [[same(row_land.at[zls[s], q, x], other) for other in by_x] for s in range(2)]
    sib_out = [same(row_land.at[zls[s], q], sibling) for s in range(2)]
    sib_parts = [(1, 0, 4), (0, 0, 2), (0, 2, 2)]
    sib_back = [
        net.make(row_grad.at[1 - q, s, pl.ds(a, n)], sib_in.at[s, pl.ds(a, n)], sibling)
        for s, a, n in sib_parts
    ]
    col_back = [
        [net.make(col_grad.at[s, o], col_in.at[s, o], by_y[o]) for o in range(3)] for s in range(2)
    ]
    row_back = [
        [net.make(row_grad.at[q, s, o], row_in.at[s, o], by_x[o]) for o in range(3)]
        for s in range(2)
    ]
    pair_back = net.make(col_grad.at[1, 3], col_last, zh_pair)
    home_sem = net.recv_sem(4)
    home = [
        pltpu.make_async_remote_copy(
            src_ref=row_grad.at[q, s, 3],
            dst_ref=row_home.at[s, q],
            send_sem=net.send_sem(),
            recv_sem=recv_sems.at[home_sem + 2 * s + q],
            device_id=source[s],
            device_id_type=MESH,
        )
        for s in range(2)
    ]

    stage1 = spread(tot1, near)

    @pl.when(is_owner)
    def _():
        start(scatter)

    start([col_pair, col_out[0][1], col_out[0][2], col_out[0][0]])
    stage1.wait()
    tot2[0] = jnp.sum(tot1[...], axis=0)
    stage2 = spread(tot2, near_x)
    scatter[0].wait_recv()
    start([row_pair, row_out[0][1], row_out[0][2], row_out[0][0]])
    stage2.wait()
    tot3[0] = jnp.sum(tot2[...], axis=0)
    stage3 = spread(tot3, near_y)
    row_grad[...] = jnp.zeros_like(row_grad)
    col_grad[...] = jnp.zeros_like(col_grad)
    col_pair.wait_recv()
    start(col_out[1])
    row_pair.wait_recv()
    start(row_out[1])
    stage3.wait()
    log_total = jnp.log(jnp.sum(tot3[...], axis=0))[:1, :1]

    def rows_of(index, count=1):
        return pl.ds(pl.multiple_of(index * share, share), count * share)

    def convert_cols(s):
        def piece(o, carry):
            at = ring(y, offset(o))
            index = s * 4 + o
            rows = rows_of(index)
            c_hi[rows, :], c_lo[rows, :] = split(col_land[zhs[s], at, pl.ds(0, share), :])
            col_log[index] = col_land[zhs[s], at, pl.ds(share, PAD), :] - log_total
            return carry

        lax.fori_loop(0, 4, piece, 0)

    def convert_rows(s):
        def piece(o, carry):
            at = ring(x, offset(o))
            index = s * 4 + o
            rows = rows_of(index)
            values = jnp.concatenate(
                [row_land[zls[s], h, at, pl.ds(0, half), :] for h in range(2)], axis=0
            )
            e_hi[rows, :], e_lo[rows, :] = split(values)
            et_hi[index], et_lo[index] = split(values.T)
            for h in range(2):
                line = row_land[zls[s], h, at, pl.ds(half, 1), pl.ds(0, half)]
                row_log[
                    pl.ds(pl.multiple_of(index * share + h * half, half), half), :
                ] = jnp.broadcast_to(line, (128, half)).T
            return carry

        lax.fori_loop(0, 4, piece, 0)

    arrive(row_out[0])
    sib_out[0].start()
    arrive(col_out[0])
    convert_cols(0)
    for copy in cooc_in:
        copy.wait()
    sib_out[0].wait_recv()
    convert_rows(0)

    entries = [tiles_ref[0, k] for k in range(4)]

    def listed(t):
        on = [jnp.where(entry == t, jnp.float32(1), jnp.float32(0)) for entry in entries]
        return (on[0] + on[1]) + (on[2] + on[3])

    def place(s):
        early = s < 8
        late = jnp.maximum(s - 8, 0)
        rs = jnp.where(early, s // 4, 1 - lax.rem(late // 2, 2))
        hr = jnp.where(early, lax.rem(s // 2, 2), lax.rem(late, 2))
        cs = jnp.where(early, 0, 1)
        hc = jnp.where(early, lax.rem(s, 2), late // 4)
        return rs, hr, cs, hc

    def score(s, slot):
        rs, hr, cs, hc = place(s)
        rows, cols = rows_of(rs * 4 + hr * 2, 2), rows_of(cs * 4 + hc * 2, 2)
        eh, ch = e_hi[rows, :], c_hi[cols, :]
        scores_v[slot] = lax.dot_general(
            jnp.concatenate([eh, eh, e_lo[rows, :]], axis=1),
            jnp.concatenate([ch, c_lo[cols, :], ch], axis=1),
            (((1,), (1,)), ((), ())),
            preferred_element_type=jnp.float32,
        )

    def work(s, slot):
        score(jnp.minimum(s + 1, 15), 1 - slot)
        rs, hr, cs, hc = place(s)
        zr, zc = jnp.where(rs == 0, blocks[0], blocks[1]), lax.rem(zh + cs, 2)
        first_row, first_col = rs * 4 + hr * 2, cs * 4 + hc * 2
        rows, cols = rows_of(first_row, 2), rows_of(first_col, 2)
        count_rows = [rows_of(zr * 4 + piece_y(ring(x, k))) for k in (2 + hr, 1 - hr)]
        count_cols = [rows_of(zc * 4 + ring(y, k)) for k in (2 + hc, 1 - hc)]
        counts = jnp.concatenate(
            [jnp.concatenate([cooc_v[r, c] for c in count_cols], axis=1) for r in count_rows],
            axis=0,
        )
        logs_row = jnp.concatenate([row_log[rows, :]] * (2 * share // 128), axis=1)
        logs_col = jnp.concatenate([col_log[first_col + k, :1, :] for k in range(2)], axis=1)
        centred = scores_v[slot] + logs_row + logs_col
        counts_f = jnp.maximum(counts.astype(jnp.float32), 1.0)
        slopes = listed(zr * 2 + zc) * jnp.where(
            counts > 0,
            (0.1 + 0.25 * jnp.sqrt(counts_f)) * (centred - jnp.log(counts_f)),
            1.0 / (1.0 + jnp.exp(-centred)),
        )
        sh, sl = split(slopes)
        ch = c_hi[cols, :]
        to_rows = jnp.dot(
            jnp.concatenate([sh, sh, sl], axis=1),
            jnp.concatenate([ch, c_lo[cols, :], ch], axis=0),
            preferred_element_type=jnp.float32,
        )
        for k in range(2):
            for h in range(2):
                start_at = k * share + h * half
                row_grad[h, rs, hr * 2 + k] += to_rows[start_at : start_at + half]
        th = jnp.concatenate([et_hi[first_row + k] for k in range(2)], axis=1)
        tl = jnp.concatenate([et_lo[first_row + k] for k in range(2)], axis=1)
        to_cols = jnp.dot(
            jnp.concatenate([th, tl, th], axis=1),
            jnp.concatenate([sh, sh, sl], axis=0),
            preferred_element_type=jnp.float32,
        )
        for k in range(2):
            col_grad[cs, hc * 2 + k] += to_cols[:, k * share : (k + 1) * share]

    def before2():
        arrive(row_out[1])
        sib_out[1].start()

    def before3():
        sib_out[1].wait_recv()
        convert_rows(1)

    def before7():
        arrive(col_out[1])
        convert_cols(1)

    def before8():
        start(col_back[0])

    def before12():
        start(col_back[1][:2])

    def before14():
        sib_back[0].start()

    def before15():
        sib_back[1].start()
        sib_back[0].wait_recv()
        row_grad[q, 1] += sib_in[1]
        start(row_back[1])

    events = {2: before2, 3: before3, 7: before7, 8: before8, 12: before12, 14: before14, 15: before15}

    score(0, 0)

    def pair(i, carry):
        for u in range(2):
            for s, event in events.items():
                if s % 2 == u:
                    pl.when(i == s // 2)(event)
            work(2 * i + u, u)
        return carry

    lax.fori_loop(0, 8, pair, 0)

    sib_back[2].start()
    col_back[1][2].start()
    sib_back[1].wait_recv()
    row_grad[q, 0, pl.ds(0, 2)] += sib_in[0, pl.ds(0, 2)]
    start(row_back[0][:2])
    sib_back[2].wait_recv()
    row_grad[q, 0, pl.ds(2, 2)] += sib_in[0, pl.ds(2, 2)]
    row_back[0][2].start()
    arrive(col_back[0])
    col_grad[0, 3] += (col_in[0, 0] + col_in[0, 1]) + col_in[0, 2]
    arrive(row_back[1])
    row_grad[q, 1, 3] += (row_in[1, 0] + row_in[1, 1]) + row_in[1, 2]

    home[1].start()
    arrive(row_back[0])
    row_grad[q, 0, 3] += (row_in[0, 0] + row_in[0, 1]) + row_in[0, 2]
    home[0].start()
    arrive(col_back[1])
    col_grad[1, 3] += (col_in[1, 0] + col_in[1, 1]) + col_in[1, 2]
    pair_back.start()
    pair_back.wait_recv()
    grad_ref[...] = (col_grad[0, 3] + col_last[...]).T

    @pl.when(is_owner)
    def _():
        for s in range(2):
            for k in range(2):
                slot = row_home.at[s, k]
                pltpu.make_async_copy(slot, slot, recv_sems.at[home_sem + 2 * s + k]).wait()
        for k in range(2):
            grad_ref[pl.ds(k * half, half), :] += row_home[0, k] + row_home[1, k]
        for copy in scatter:
            copy.wait_send()

    for copy in home:
        copy.wait_send()
    net.finish()


def local(cooc, tile_list, marginal, embed, accum):
    share, width = embed.shape
    half = share // 2
    items = 8 * share
    f32, bf16 = jnp.float32, jnp.bfloat16
    hbm = pl.BlockSpec(memory_space=pl.ANY)
    vmem = pl.BlockSpec(memory_space=pltpu.VMEM)
    smem = pl.BlockSpec(memory_space=pltpu.SMEM)
    summed = pl.pallas_call(
        kernel,
        out_shape=jax.ShapeDtypeStruct((share, width), f32),
        in_specs=[hbm, vmem, smem, hbm],
        out_specs=vmem,
        scratch_shapes=[
            pltpu.VMEM((2, 4, share + PAD, width), f32),
            pltpu.VMEM((2, 2, 4, half + PAD, width), f32),
            pltpu.VMEM((2, half + PAD, width), f32),
            pltpu.VMEM((items, items), jnp.int32),
            pltpu.VMEM((items, width), bf16),
            pltpu.VMEM((items, width), bf16),
            pltpu.VMEM((8, width, share), bf16),
            pltpu.VMEM((8, width, share), bf16),
            pltpu.VMEM((items, width), bf16),
            pltpu.VMEM((items, width), bf16),
            pltpu.VMEM((items, 128), f32),
            pltpu.VMEM((8, PAD, share), f32),
            pltpu.VMEM((2, 2 * share, 2 * share), f32),
            pltpu.VMEM((2, 2, 4, half, width), f32),
            pltpu.VMEM((2, 4, width, share), f32),
            pltpu.VMEM((2, 4, half, width), f32),
            pltpu.VMEM((2, 3, half, width), f32),
            pltpu.VMEM((2, 2, half, width), f32),
            pltpu.VMEM((2, 3, width, share), f32),
            pltpu.VMEM((width, share), f32),
            pltpu.VMEM((8, 8, 128), f32),
            pltpu.VMEM((4, 8, 128), f32),
            pltpu.VMEM((4, 8, 128), f32),
            pltpu.SemaphoreType.DMA((N_SEND,)),
            pltpu.SemaphoreType.DMA((N_RECV,)),
            pltpu.SemaphoreType.DMA((9,)),
        ],
        compiler_params=pltpu.CompilerParams(
            collective_id=0, has_side_effects=True, vmem_limit_bytes=56 * 2**20
        ),
        cost_estimate=pl.CostEstimate(
            flops=18 * items * items * width, bytes_accessed=4 * items * items, transcendentals=0
        ),
    )(embed, marginal.reshape(1, share), tile_list.reshape(1, 4), cooc)
    gradients = summed / (items // 2)
    new_accum = accum + gradients * gradients
    new_embed = embed - LEARN_RATE * gradients / jnp.sqrt(new_accum)
    return (new_embed, new_accum)


def solution(mesh):
    placed = (
        P("row", "col"),
        P("row", "col", None),
        P(("col", "row")),
        P(("col", "row"), None),
        P(("col", "row"), None),
    )
    return jax.shard_map(
        local,
        mesh=mesh,
        in_specs=placed,
        out_specs=(P(("col", "row"), None), P(("col", "row"), None)),
        check_vma=False,
    )
```

```python
import jax
import jax.numpy as jnp
from jax import lax
from jax.experimental import pallas as pl
from jax.experimental.pallas import tpu as pltpu
from jax.sharding import PartitionSpec as P

LEARN_RATE = 0.05
MESH = pl.DeviceIdType.MESH
PAD = 8
RING = 4
N_SEND = 64
N_RECV = 48


def split(value):
    high = value.astype(jnp.bfloat16)
    low = (value - high.astype(jnp.float32)).astype(jnp.bfloat16)
    return high, low


class Copies:
    def __init__(self, send_sems, recv_sems):
        self.send_sems, self.recv_sems = send_sems, recv_sems
        self.sends = self.recvs = 0
        self.pending = []

    def send_sem(self):
        self.sends += 1
        return self.send_sems.at[self.sends - 1]

    def recv_sem(self, count=1):
        self.recvs += count
        return self.recvs - count

    def make(self, src, dst, device):
        copy = pltpu.make_async_remote_copy(
            src_ref=src,
            dst_ref=dst,
            send_sem=self.send_sem(),
            recv_sem=self.recv_sems.at[self.recv_sem()],
            device_id=device,
            device_id_type=MESH,
        )
        self.pending.append(copy)
        return copy

    def finish(self):
        for copy in self.pending:
            copy.wait_send()


def kernel(
    embed_hbm,
    marg_ref,
    tiles_ref,
    cooc_hbm,
    grad_ref,
    col_land,
    row_land,
    row_src,
    cooc_v,
    e_hi,
    e_lo,
    et_hi,
    et_lo,
    c_hi,
    c_lo,
    row_log,
    col_log,
    scores_v,
    row_grad,
    col_grad,
    sib_in,
    row_in,
    row_feed,
    row_home,
    col_in,
    col_last,
    tot1,
    tot2,
    tot3,
    send_sems,
    recv_sems,
    local_sems,
):
    share, width = embed_hbm.shape
    half = share // 2
    row = lax.axis_index("row")
    col = lax.axis_index("col")
    zh, y = row // 4, lax.rem(row, 4)
    x, zl, q = col // 4, lax.rem(col // 2, 2), lax.rem(col, 2)

    def device(zh_=zh, y_=y, x_=x, zl_=zl, q_=q):
        return (zh_ * 4 + y_, x_ * 4 + zl_ * 2 + q_)

    def ring(position, step):
        return lax.rem(position + step + RING, RING)

    def offset(o):
        return jnp.where(o == 0, 2, jnp.where(o == 1, 1, jnp.where(o == 2, 3, 0)))

    is_owner = col < 8

    def flip(bit, by):
        return 1 - bit if by else bit

    near = [
        device(zh_=flip(zh, k // 4), zl_=flip(zl, k // 2 % 2), q_=flip(q, k % 2))
        for k in range(1, 8)
    ]
    near_y = [device(y_=ring(y, k)) for k in range(1, 4)]
    near_x = [device(x_=ring(x, k)) for k in range(1, 4)]
    by_y = [near_y[1], near_y[0], near_y[2]]
    by_x = [near_x[1], near_x[0], near_x[2]]
    sibling, zl_pair, zh_pair = near[0], near[1], near[3]
    blocks = [lax.rem(zh + zl + s + y // 2, 2) for s in range(2)]

    def piece_y(x_, h):
        return lax.rem(zh + 1 + 2 * h + y - x_ + RING, RING)

    source = [(blocks[s] * 4 + piece_y(x, q), row) for s in range(2)]
    relay_self = jnp.logical_and(source[0][0] == row, x * 4 + y == col)
    x_place = [lax.rem(x + 1 + 2 * k - y + zl * 2 + q + RING, RING) for k in range(2)]
    zl_place = lax.rem(zl + zh + x, 2)
    targets = [(col, x_place[k] * 4 + zl_place * 2 + k) for k in range(2)]
    relay = [(source[s][0], x * 4 + y) for s in range(2)]
    relay_y = zl * 2 + q
    turn = lax.rem(x + 3 + y - relay_y + RING, RING)
    back_zh, back_h = lax.rem(turn, 2), turn // 2
    back_zl = lax.rem(zl + zh + back_zh, 2)
    feeders = [
        (back_zh * 4 + relay_y, x * 4 + lax.rem(back_zl + s, 2) * 2 + back_h) for s in range(2)
    ]
    feeds_self = jnp.logical_and(feeders[0][0] == row, feeders[0][1] == col)

    embed_in = pltpu.make_async_copy(
        embed_hbm, col_land.at[zh, y, pl.ds(0, share)], local_sems.at[0]
    )
    embed_in.start()
    cooc_in = [
        pltpu.make_async_copy(
            cooc_hbm.at[pl.ds(p * share, share)],
            cooc_v.at[pl.ds(p * share, share)],
            local_sems.at[1 + p],
        )
        for p in range(8)
    ]

    def start_cooc():
        for copy in cooc_in:
            copy.start()

    def signal(other):
        pl.semaphore_signal(barrier, inc=1, device_id=other, device_id_type=MESH)

    barrier = pltpu.get_barrier_semaphore()
    for other in near + near_y + near_x + [source[0], feeders[1]]:
        signal(other)

    @pl.when(jnp.logical_not(feeds_self))
    def _():
        signal(feeders[0])

    marg = marg_ref[...].astype(jnp.float32)
    logs = jnp.log(marg)
    tot1[0] = jnp.broadcast_to(jnp.sum(marg, axis=1, keepdims=True), tot1.shape[1:])
    embed_in.wait()
    col_land[zh, y, pl.ds(share, PAD), :] = jnp.broadcast_to(logs, (PAD, width))
    for h in range(2):
        row_src[h, pl.ds(0, half), :] = col_land[zh, y, pl.ds(h * half, half), :]
        row_src[h, pl.ds(half, PAD), :] = jnp.broadcast_to(
            jnp.concatenate([logs[:, h * half : (h + 1) * half]] * 2, axis=1), (PAD, width)
        )

    pl.semaphore_wait(barrier, 14 + jnp.where(relay_self, 0, 1) + jnp.where(is_owner, 2, 0))

    net = Copies(send_sems, recv_sems)

    def spread(block_ref, others):
        sem = recv_sems.at[net.recv_sem()]
        for k, other in enumerate(others):
            copy = pltpu.make_async_remote_copy(
                src_ref=block_ref.at[0],
                dst_ref=block_ref.at[k + 1],
                send_sem=net.send_sem(),
                recv_sem=sem,
                device_id=other,
                device_id_type=MESH,
            )
            copy.start()
            net.pending.append(copy)
        landed = block_ref.at[pl.ds(1, len(others))]
        return pltpu.make_async_copy(landed, landed, sem)

    def same(ref, other):
        return net.make(ref, ref, other)

    def start(copies):
        for copy in copies:
            copy.start()

    def arrive(copies):
        for copy in copies:
            copy.wait_recv()

    zls, zhs = (zl, 1 - zl), (zh, 1 - zh)
    scatter_recv = recv_sems.at[net.recv_sem()]
    scatter = [
        pltpu.make_async_remote_copy(
            src_ref=row_src.at[k],
            dst_ref=row_land.at[zl_place, k, x_place[k]],
            send_sem=net.send_sem(),
            recv_sem=scatter_recv,
            device_id=targets[k],
            device_id_type=MESH,
        )
        for k in range(2)
    ]
    col_pair = same(col_land.at[zh, y], zh_pair)
    row_pair = same(row_land.at[zl, q, x], zl_pair)
    col_out = [[same(col_land.at[zhs[s], y], other) for other in by_y[1:]] for s in range(2)]
    upper, lower = pl.ds(0, half + PAD), pl.ds(half + PAD, half)
    col_relay = [
        same(col_land.at[zh, ring(y, -1), upper], by_y[1]),
        same(col_land.at[zh, ring(y, 1), lower], by_y[2]),
    ]
    col_far = same(col_land.at[zh, ring(y, 2)], zh_pair)
    row_out = [[same(row_land.at[zls[s], q, x], other) for other in by_x] for s in range(2)]
    sib_out = [same(row_land.at[zls[s], q], sibling) for s in range(2)]
    sib_parts = [(1, 0, 4), (0, 0, 2), (0, 2, 2)]
    sib_back = [
        net.make(row_grad.at[1 - q, s, pl.ds(a, n)], sib_in.at[s, pl.ds(a, n)], sibling)
        for s, a, n in sib_parts
    ]
    col_back = [
        [net.make(col_grad.at[0, o], col_in.at[0, o], by_y[o]) for o in range(3)],
        [net.make(col_grad.at[1, o], col_in.at[1, o], by_y[o]) for o in (1, 2)],
    ]
    far_back = net.make(col_grad.at[1, 0], col_in.at[1, 0], zh_pair)
    row_back = [
        [net.make(row_grad.at[q, s, o], row_in.at[s, o], by_x[o]) for o in range(3)]
        for s in range(2)
    ]
    pair_back = net.make(col_grad.at[1, 3], col_last, zh_pair)
    feed_sem = net.recv_sem(2)
    feed = [
        pltpu.make_async_remote_copy(
            src_ref=row_grad.at[q, s, 3],
            dst_ref=row_feed.at[s],
            send_sem=net.send_sem(),
            recv_sem=recv_sems.at[feed_sem + s],
            device_id=relay[s],
            device_id_type=MESH,
        )
        for s in range(2)
    ]
    feed_here = pltpu.make_async_copy(
        row_grad.at[q, 0, 3], row_feed.at[0], recv_sems.at[feed_sem]
    )
    home_sem = net.recv_sem(2)
    home = pltpu.make_async_remote_copy(
        src_ref=row_feed.at[0],
        dst_ref=row_home.at[back_h],
        send_sem=net.send_sem(),
        recv_sem=recv_sems.at[home_sem + back_h],
        device_id=device(x_=back_zh),
        device_id_type=MESH,
    )
    ends_here = x == back_zh

    @pl.when(is_owner)
    def _():
        start(scatter)

    start(col_out[0])
    stage1 = spread(tot1, near)
    start_cooc()
    row_grad[...] = jnp.zeros_like(row_grad)
    col_grad[...] = jnp.zeros_like(col_grad)
    stage1.wait()
    tot2[0] = jnp.sum(tot1[...], axis=0)
    stage2 = spread(tot2, near_x)
    scatter[0].wait_recv()
    start([row_out[0][1], row_out[0][2], row_out[0][0], row_pair, col_pair])
    stage2.wait()
    tot3[0] = jnp.sum(tot2[...], axis=0)
    stage3 = spread(tot3, near_y)
    col_out[0][0].wait_recv()
    col_relay[0].start()
    col_out[0][1].wait_recv()
    col_relay[1].start()
    arrive(row_out[0])
    sib_out[0].start()
    row_pair.wait_recv()
    start(row_out[1])
    stage3.wait()
    log_total = jnp.log(jnp.sum(tot3[...], axis=0))[:1, :1]

    def rows_of(index, count=1):
        return pl.ds(pl.multiple_of(index * share, share), count * share)

    def convert_cols(s):
        def piece(o, carry):
            at = ring(y, offset(o))
            index = s * 4 + o
            rows = rows_of(index)
            c_hi[rows, :], c_lo[rows, :] = split(col_land[zhs[s], at, pl.ds(0, share), :])
            col_log[index] = col_land[zhs[s], at, pl.ds(share, PAD), :] - log_total
            return carry

        lax.fori_loop(0, 4, piece, 0)

    def convert_rows(s):
        def piece(o, carry):
            at = ring(x, offset(o))
            index = s * 4 + o
            rows = rows_of(index)
            values = jnp.concatenate(
                [row_land[zls[s], h, at, pl.ds(0, half), :] for h in range(2)], axis=0
            )
            e_hi[rows, :], e_lo[rows, :] = split(values)
            et_hi[index], et_lo[index] = split(values.T)
            for h in range(2):
                line = row_land[zls[s], h, at, pl.ds(half, 1), pl.ds(0, half)]
                row_log[
                    pl.ds(pl.multiple_of(index * share + h * half, half), half), :
                ] = jnp.broadcast_to(line, (128, half)).T
            return carry

        lax.fori_loop(0, 4, piece, 0)

    arrive(col_relay)
    col_far.start()
    col_pair.wait_recv()
    start(col_out[1])
    convert_cols(0)
    for copy in cooc_in:
        copy.wait()
    sib_out[0].wait_recv()
    convert_rows(0)

    entries = [tiles_ref[0, k] for k in range(4)]

    def listed(t):
        on = [jnp.where(entry == t, jnp.float32(1), jnp.float32(0)) for entry in entries]
        return (on[0] + on[1]) + (on[2] + on[3])

    def place(s):
        early = s < 8
        late = jnp.maximum(s - 8, 0)
        rs = jnp.where(early, s // 4, 1 - late // 4)
        by_row = jnp.logical_or(early, s >= 12)
        hr = lax.rem(jnp.where(by_row, s // 2, s), 2)
        cs = jnp.where(early, 0, 1)
        hc = lax.rem(jnp.where(by_row, s, s // 2), 2)
        return rs, hr, cs, hc

    def score(s, slot):
        rs, hr, cs, hc = place(s)
        rows, cols = rows_of(rs * 4 + hr * 2, 2), rows_of(cs * 4 + hc * 2, 2)
        eh, ch = e_hi[rows, :], c_hi[cols, :]
        scores_v[slot] = lax.dot_general(
            jnp.concatenate([eh, eh, e_lo[rows, :]], axis=1),
            jnp.concatenate([ch, c_lo[cols, :], ch], axis=1),
            (((1,), (1,)), ((), ())),
            preferred_element_type=jnp.float32,
        )

    def work(s, slot):
        score(jnp.minimum(s + 1, 15), 1 - slot)
        rs, hr, cs, hc = place(s)
        zr, zc = jnp.where(rs == 0, blocks[0], blocks[1]), lax.rem(zh + cs, 2)
        first_row, first_col = rs * 4 + hr * 2, cs * 4 + hc * 2
        rows, cols = rows_of(first_row, 2), rows_of(first_col, 2)
        count_rows = [
            pl.ds(
                pl.multiple_of((zr * 4 + piece_y(ring(x, k), h)) * share + h * half, half), half
            )
            for k in (2 + hr, 1 - hr)
            for h in range(2)
        ]
        count_cols = [rows_of(zc * 4 + ring(y, k)) for k in (2 + hc, 1 - hc)]
        counts = jnp.concatenate(
            [jnp.concatenate([cooc_v[r, c] for c in count_cols], axis=1) for r in count_rows],
            axis=0,
        )
        logs_row = jnp.concatenate([row_log[rows, :]] * (2 * share // 128), axis=1)
        logs_col = jnp.concatenate([col_log[first_col + k, :1, :] for k in range(2)], axis=1)
        centred = scores_v[slot] + logs_row + logs_col
        counts_f = jnp.maximum(counts.astype(jnp.float32), 1.0)
        slopes = listed(zr * 2 + zc) * jnp.where(
            counts > 0,
            (0.1 + 0.25 * jnp.sqrt(counts_f)) * (centred - jnp.log(counts_f)),
            1.0 / (1.0 + jnp.exp(-centred)),
        )
        sh, sl = split(slopes)
        ch = c_hi[cols, :]
        to_rows = jnp.dot(
            jnp.concatenate([sh, sh, sl], axis=1),
            jnp.concatenate([ch, c_lo[cols, :], ch], axis=0),
            preferred_element_type=jnp.float32,
        )
        for k in range(2):
            for h in range(2):
                start_at = k * share + h * half
                row_grad[h, rs, hr * 2 + k] += to_rows[start_at : start_at + half]
        th = jnp.concatenate([et_hi[first_row + k] for k in range(2)], axis=1)
        tl = jnp.concatenate([et_lo[first_row + k] for k in range(2)], axis=1)
        to_cols = jnp.dot(
            jnp.concatenate([th, tl, th], axis=1),
            jnp.concatenate([sh, sh, sl], axis=0),
            preferred_element_type=jnp.float32,
        )
        for k in range(2):
            col_grad[cs, hc * 2 + k] += to_cols[:, k * share : (k + 1) * share]

    def before2():
        arrive(row_out[1])
        sib_out[1].start()

    def before3():
        sib_out[1].wait_recv()
        convert_rows(1)

    def before7():
        arrive(col_out[1])
        col_far.wait_recv()
        convert_cols(1)

    def before8():
        start(col_back[0][1:])

    def before12():
        sib_back[0].start()

    def before13():
        sib_back[0].wait_recv()
        row_grad[q, 1] += sib_in[1]
        start(row_back[1])

    def before14():
        sib_back[1].start()

    def before15():
        far_back.start()
        col_back[1][0].start()
        sib_back[1].wait_recv()
        row_grad[q, 0, pl.ds(0, 2)] += sib_in[0, pl.ds(0, 2)]
        start(row_back[0][:2])

    events = {
        2: before2,
        3: before3,
        7: before7,
        8: before8,
        12: before12,
        13: before13,
        14: before14,
        15: before15,
    }

    score(0, 0)

    def pair(i, carry):
        for u in range(2):
            for s, event in events.items():
                if s % 2 == u:
                    pl.when(i == s // 2)(event)
            work(2 * i + u, u)
        return carry

    lax.fori_loop(0, 8, pair, 0)

    sib_back[2].start()
    col_back[1][1].start()
    arrive(row_back[1])
    row_grad[q, 1, 3] += (row_in[1, 0] + row_in[1, 1]) + row_in[1, 2]
    feed[1].start()
    sib_back[2].wait_recv()
    row_grad[q, 0, pl.ds(2, 2)] += sib_in[0, pl.ds(2, 2)]
    row_back[0][2].start()
    far_back.wait_recv()
    col_grad[0, 0] += col_in[1, 0]
    col_back[0][0].start()
    arrive(row_back[0])
    row_grad[q, 0, 3] += (row_in[0, 0] + row_in[0, 1]) + row_in[0, 2]

    @pl.when(relay_self)
    def _():
        feed_here.start()

    @pl.when(jnp.logical_not(relay_self))
    def _():
        feed[0].start()

    arrive(col_back[1])
    col_grad[1, 3] += col_in[1, 1] + col_in[1, 2]
    pair_back.start()
    for s in range(2):
        slot = row_feed.at[s]
        pltpu.make_async_copy(slot, slot, recv_sems.at[feed_sem + s]).wait()
    row_feed[0] += row_feed[1]

    @pl.when(jnp.logical_not(ends_here))
    def _():
        home.start()

    arrive(col_back[0])
    col_grad[0, 3] += (col_in[0, 0] + col_in[0, 1]) + col_in[0, 2]
    pair_back.wait_recv()
    grad_ref[...] = (col_grad[0, 3] + col_last[...]).T

    @pl.when(is_owner)
    def _():
        for k in range(2):
            part = pl.ds(k * half, half)

            @pl.when(x_place[k] == x)
            def _():
                grad_ref[part, :] += row_feed[0]

            @pl.when(x_place[k] != x)
            def _():
                slot = row_home.at[k]
                pltpu.make_async_copy(slot, slot, recv_sems.at[home_sem + k]).wait()
                grad_ref[part, :] += row_home[k]

        for copy in scatter:
            copy.wait_send()

    @pl.when(jnp.logical_not(relay_self))
    def _():
        feed[0].wait_send()

    feed[1].wait_send()

    @pl.when(jnp.logical_not(ends_here))
    def _():
        home.wait_send()

    net.finish()


def local(cooc, tile_list, marginal, embed, accum):
    share, width = embed.shape
    half = share // 2
    items = 8 * share
    f32, bf16 = jnp.float32, jnp.bfloat16
    hbm = pl.BlockSpec(memory_space=pl.ANY)
    vmem = pl.BlockSpec(memory_space=pltpu.VMEM)
    smem = pl.BlockSpec(memory_space=pltpu.SMEM)
    summed = pl.pallas_call(
        kernel,
        out_shape=jax.ShapeDtypeStruct((share, width), f32),
        in_specs=[hbm, vmem, smem, hbm],
        out_specs=vmem,
        scratch_shapes=[
            pltpu.VMEM((2, 4, share + PAD, width), f32),
            pltpu.VMEM((2, 2, 4, half + PAD, width), f32),
            pltpu.VMEM((2, half + PAD, width), f32),
            pltpu.VMEM((items, items), jnp.int32),
            pltpu.VMEM((items, width), bf16),
            pltpu.VMEM((items, width), bf16),
            pltpu.VMEM((8, width, share), bf16),
            pltpu.VMEM((8, width, share), bf16),
            pltpu.VMEM((items, width), bf16),
            pltpu.VMEM((items, width), bf16),
            pltpu.VMEM((items, 128), f32),
            pltpu.VMEM((8, PAD, share), f32),
            pltpu.VMEM((2, 2 * share, 2 * share), f32),
            pltpu.VMEM((2, 2, 4, half, width), f32),
            pltpu.VMEM((2, 4, width, share), f32),
            pltpu.VMEM((2, 4, half, width), f32),
            pltpu.VMEM((2, 3, half, width), f32),
            pltpu.VMEM((2, half, width), f32),
            pltpu.VMEM((2, half, width), f32),
            pltpu.VMEM((2, 3, width, share), f32),
            pltpu.VMEM((width, share), f32),
            pltpu.VMEM((8, 8, 128), f32),
            pltpu.VMEM((4, 8, 128), f32),
            pltpu.VMEM((4, 8, 128), f32),
            pltpu.SemaphoreType.DMA((N_SEND,)),
            pltpu.SemaphoreType.DMA((N_RECV,)),
            pltpu.SemaphoreType.DMA((9,)),
        ],
        compiler_params=pltpu.CompilerParams(
            collective_id=0, has_side_effects=True, vmem_limit_bytes=56 * 2**20
        ),
        cost_estimate=pl.CostEstimate(
            flops=18 * items * items * width, bytes_accessed=4 * items * items, transcendentals=0
        ),
    )(embed, marginal.reshape(1, share), tile_list.reshape(1, 4), cooc)
    gradients = summed / (items // 2)
    new_accum = accum + gradients * gradients
    new_embed = embed - LEARN_RATE * gradients / jnp.sqrt(new_accum)
    return (new_embed, new_accum)


def solution(mesh):
    placed = (
        P("row", "col"),
        P("row", "col", None),
        P(("col", "row")),
        P(("col", "row"), None),
        P(("col", "row"), None),
    )
    return jax.shard_map(
        local,
        mesh=mesh,
        in_specs=placed,
        out_specs=(P(("col", "row"), None), P(("col", "row"), None)),
        check_vma=False,
    )
```

```python
import jax
import jax.numpy as jnp
from jax import lax
from jax.experimental import pallas as pl
from jax.experimental.pallas import tpu as pltpu
from jax.sharding import PartitionSpec as P

LEARN_RATE = 0.05
MESH = pl.DeviceIdType.MESH
PAD = 8
RING = 4
N_SEND = 64
N_RECV = 48


def split(value):
    high = value.astype(jnp.bfloat16)
    low = (value - high.astype(jnp.float32)).astype(jnp.bfloat16)
    return high, low


class Copies:
    def __init__(self, send_sems, recv_sems):
        self.send_sems, self.recv_sems = send_sems, recv_sems
        self.sends = self.recvs = 0
        self.pending = []

    def send_sem(self):
        self.sends += 1
        return self.send_sems.at[self.sends - 1]

    def recv_sem(self, count=1):
        self.recvs += count
        return self.recvs - count

    def make(self, src, dst, device):
        copy = pltpu.make_async_remote_copy(
            src_ref=src,
            dst_ref=dst,
            send_sem=self.send_sem(),
            recv_sem=self.recv_sems.at[self.recv_sem()],
            device_id=device,
            device_id_type=MESH,
        )
        self.pending.append(copy)
        return copy

    def finish(self):
        for copy in self.pending:
            copy.wait_send()


def kernel(
    embed_hbm,
    marg_ref,
    tiles_ref,
    cooc_hbm,
    grad_ref,
    col_land,
    row_land,
    row_src,
    cooc_v,
    e_hi,
    e_lo,
    et_hi,
    et_lo,
    c_hi,
    c_lo,
    row_log,
    col_log,
    scores_v,
    row_grad,
    col_grad,
    sib_in,
    row_in,
    row_feed,
    row_home,
    col_in,
    col_last,
    tot1,
    tot2,
    tot3,
    send_sems,
    recv_sems,
    local_sems,
):
    share, width = embed_hbm.shape
    half = share // 2
    row = lax.axis_index("row")
    col = lax.axis_index("col")
    zh, y = row // 4, lax.rem(row, 4)
    x, zl, q = col // 4, lax.rem(col // 2, 2), lax.rem(col, 2)

    def device(zh_=zh, y_=y, x_=x, zl_=zl, q_=q):
        return (zh_ * 4 + y_, x_ * 4 + zl_ * 2 + q_)

    def ring(position, step):
        return lax.rem(position + step + RING, RING)

    def offset(o):
        return jnp.where(o == 0, 1, jnp.where(o == 1, 3, jnp.where(o == 2, 2, 0)))

    is_owner = col < 8

    def flip(bit, by):
        return 1 - bit if by else bit

    near = [
        device(zh_=flip(zh, k // 4), zl_=flip(zl, k // 2 % 2), q_=flip(q, k % 2))
        for k in range(1, 8)
    ]
    near_y = [device(y_=ring(y, k)) for k in range(1, 4)]
    near_x = [device(x_=ring(x, k)) for k in range(1, 4)]
    by_y = [near_y[0], near_y[2], near_y[1]]
    by_x = [near_x[0], near_x[2], near_x[1]]
    sibling, zl_pair, zh_pair = near[0], near[1], near[3]
    blocks = [lax.rem(zh + zl + s + y // 2, 2) for s in range(2)]

    def piece_y(x_, h):
        return lax.rem(zh + 1 + 2 * h + y - x_ + RING, RING)

    source = [(blocks[s] * 4 + piece_y(x, q), row) for s in range(2)]
    relay_self = jnp.logical_and(source[0][0] == row, x * 4 + y == col)
    x_place = [lax.rem(x + 1 + 2 * k - y + zl * 2 + q + RING, RING) for k in range(2)]
    zl_place = lax.rem(zl + zh + x, 2)
    targets = [(col, x_place[k] * 4 + zl_place * 2 + k) for k in range(2)]
    relay = [(source[s][0], x * 4 + y) for s in range(2)]
    relay_y = zl * 2 + q
    turn = lax.rem(x + 3 + y - relay_y + RING, RING)
    back_zh, back_h = lax.rem(turn, 2), turn // 2
    back_zl = lax.rem(zl + zh + back_zh, 2)
    feeders = [
        (back_zh * 4 + relay_y, x * 4 + lax.rem(back_zl + s, 2) * 2 + back_h) for s in range(2)
    ]
    feeds_self = jnp.logical_and(feeders[0][0] == row, feeders[0][1] == col)

    embed_in = pltpu.make_async_copy(
        embed_hbm, col_land.at[zh, y, pl.ds(0, share)], local_sems.at[0]
    )
    embed_in.start()
    cooc_in = [
        pltpu.make_async_copy(
            cooc_hbm.at[pl.ds(p * share, share)],
            cooc_v.at[pl.ds(p * share, share)],
            local_sems.at[1 + p],
        )
        for p in range(8)
    ]

    for copy in cooc_in:
        copy.start()

    def signal(other):
        pl.semaphore_signal(barrier, inc=1, device_id=other, device_id_type=MESH)

    barrier = pltpu.get_barrier_semaphore()
    for other in near + near_y + near_x + [source[0], feeders[1]]:
        signal(other)

    @pl.when(jnp.logical_not(feeds_self))
    def _():
        signal(feeders[0])

    marg = marg_ref[...].astype(jnp.float32)
    logs = jnp.log(marg)
    tot1[0] = jnp.broadcast_to(jnp.sum(marg, axis=1, keepdims=True), tot1.shape[1:])
    embed_in.wait()
    col_land[zh, y, pl.ds(share, PAD), :] = jnp.broadcast_to(logs, (PAD, width))
    for h in range(2):
        row_src[h, pl.ds(0, half), :] = col_land[zh, y, pl.ds(h * half, half), :]
        row_src[h, pl.ds(half, PAD), :] = jnp.broadcast_to(
            jnp.concatenate([logs[:, h * half : (h + 1) * half]] * 2, axis=1), (PAD, width)
        )

    pl.semaphore_wait(barrier, 14 + jnp.where(relay_self, 0, 1) + jnp.where(is_owner, 2, 0))

    net = Copies(send_sems, recv_sems)

    def spread(block_ref, others):
        sem = recv_sems.at[net.recv_sem()]
        for k, other in enumerate(others):
            copy = pltpu.make_async_remote_copy(
                src_ref=block_ref.at[0],
                dst_ref=block_ref.at[k + 1],
                send_sem=net.send_sem(),
                recv_sem=sem,
                device_id=other,
                device_id_type=MESH,
            )
            copy.start()
            net.pending.append(copy)
        landed = block_ref.at[pl.ds(1, len(others))]
        return pltpu.make_async_copy(landed, landed, sem)

    def same(ref, other):
        return net.make(ref, ref, other)

    def start(copies):
        for copy in copies:
            copy.start()

    def arrive(copies):
        for copy in copies:
            copy.wait_recv()

    zls, zhs = (zl, 1 - zl), (zh, 1 - zh)
    scatter_recv = recv_sems.at[net.recv_sem()]
    scatter = [
        pltpu.make_async_remote_copy(
            src_ref=row_src.at[k],
            dst_ref=row_land.at[zl_place, k, x_place[k]],
            send_sem=net.send_sem(),
            recv_sem=scatter_recv,
            device_id=targets[k],
            device_id_type=MESH,
        )
        for k in range(2)
    ]
    col_pair = same(col_land.at[zh, y], zh_pair)
    row_pair = same(row_land.at[zl, q, x], zl_pair)
    col_out = [[same(col_land.at[zhs[s], y], other) for other in by_y[:2]] for s in range(2)]
    upper, lower = pl.ds(0, half + PAD), pl.ds(half + PAD, half)
    col_relay = [
        same(col_land.at[zh, ring(y, -1), upper], by_y[0]),
        same(col_land.at[zh, ring(y, 1), lower], by_y[1]),
    ]
    col_far = same(col_land.at[zh, ring(y, 2)], zh_pair)
    row_out = [[same(row_land.at[zls[s], q, x], other) for other in by_x] for s in range(2)]
    sib_pieces = [same(row_land.at[zl, q, ring(x, step)], sibling) for step in (1, 3, 2, 0)]
    sib_block = same(row_land.at[1 - zl, q], sibling)
    sib_parts = [(0, 0, 4), (1, 0, 2), (1, 2, 2)]
    sib_back = [
        net.make(row_grad.at[1 - q, s, pl.ds(a, n)], sib_in.at[s, pl.ds(a, n)], sibling)
        for s, a, n in sib_parts
    ]
    col_back = [
        [net.make(col_grad.at[0, o], col_in.at[0, o], by_y[o]) for o in range(3)],
        [net.make(col_grad.at[1, o], col_in.at[1, o], by_y[o]) for o in range(2)],
    ]
    far_back = net.make(col_grad.at[1, 2], col_in.at[1, 2], zh_pair)
    row_back = [
        [net.make(row_grad.at[q, s, o], row_in.at[s, o], by_x[o]) for o in range(3)]
        for s in range(2)
    ]
    pair_back = net.make(col_grad.at[1, 3], col_last, zh_pair)
    feed_sem = net.recv_sem(2)
    feed = [
        pltpu.make_async_remote_copy(
            src_ref=row_grad.at[q, s, 3],
            dst_ref=row_feed.at[s],
            send_sem=net.send_sem(),
            recv_sem=recv_sems.at[feed_sem + s],
            device_id=relay[s],
            device_id_type=MESH,
        )
        for s in range(2)
    ]
    feed_here = pltpu.make_async_copy(
        row_grad.at[q, 0, 3], row_feed.at[0], recv_sems.at[feed_sem]
    )
    home_sem = net.recv_sem(2)
    home = pltpu.make_async_remote_copy(
        src_ref=row_feed.at[0],
        dst_ref=row_home.at[back_h],
        send_sem=net.send_sem(),
        recv_sem=recv_sems.at[home_sem + back_h],
        device_id=device(x_=back_zh),
        device_id_type=MESH,
    )
    ends_here = x == back_zh

    @pl.when(is_owner)
    def _():
        start(scatter)

    start(col_out[0])
    stage1 = spread(tot1, near)
    row_grad[...] = jnp.zeros_like(row_grad)
    col_grad[...] = jnp.zeros_like(col_grad)
    stage1.wait()
    tot2[0] = jnp.sum(tot1[...], axis=0)
    stage2 = spread(tot2, near_x)
    scatter[0].wait_recv()
    start([*row_out[0][:2], sib_pieces[3], row_out[0][2], row_pair, col_pair])
    stage2.wait()
    tot3[0] = jnp.sum(tot2[...], axis=0)
    stage3 = spread(tot3, near_y)
    col_out[0][0].wait_recv()
    col_relay[0].start()
    col_out[0][1].wait_recv()
    col_relay[1].start()
    for k in range(2):
        row_out[0][k].wait_recv()
        sib_pieces[1 - k].start()
    stage3.wait()
    log_total = jnp.log(jnp.sum(tot3[...], axis=0))[:1, :1]

    def rows_of(index, count=1):
        return pl.ds(pl.multiple_of(index * share, share), count * share)

    def convert_cols(s, first, last):
        def piece(o, carry):
            at = ring(y, offset(o))
            index = s * 4 + o
            rows = rows_of(index)
            c_hi[rows, :], c_lo[rows, :] = split(col_land[zhs[s], at, pl.ds(0, share), :])
            col_log[index] = col_land[zhs[s], at, pl.ds(share, PAD), :] - log_total
            return carry

        lax.fori_loop(first, last, piece, 0)

    def convert_rows(s, first, last):
        def piece(o, carry):
            at = ring(x, offset(o))
            index = s * 4 + o
            rows = rows_of(index)
            values = jnp.concatenate(
                [row_land[zls[s], h, at, pl.ds(0, half), :] for h in range(2)], axis=0
            )
            e_hi[rows, :], e_lo[rows, :] = split(values)
            et_hi[index], et_lo[index] = split(values.T)
            for h in range(2):
                line = row_land[zls[s], h, at, pl.ds(half, 1), pl.ds(0, half)]
                row_log[
                    pl.ds(pl.multiple_of(index * share + h * half, half), half), :
                ] = jnp.broadcast_to(line, (128, half)).T
            return carry

        lax.fori_loop(first, last, piece, 0)

    arrive(col_relay)
    col_far.start()
    col_pair.wait_recv()
    start(col_out[1])
    convert_cols(0, 0, 4)
    arrive(sib_pieces[:2])
    convert_rows(0, 0, 2)
    row_out[0][2].wait_recv()
    sib_pieces[2].start()
    row_pair.wait_recv()
    start(row_out[1])
    for copy in cooc_in:
        copy.wait()

    entries = [tiles_ref[0, k] for k in range(4)]

    def listed(t):
        on = [jnp.where(entry == t, jnp.float32(1), jnp.float32(0)) for entry in entries]
        return (on[0] + on[1]) + (on[2] + on[3])

    def place(s):
        rs = s // 8
        cs = jnp.where(jnp.logical_and(s >= 4, s < 12), 1, 0)
        by_row = jnp.logical_or(s < 8, s >= 12)
        hr = lax.rem(jnp.where(by_row, s // 2, s), 2)
        hc = lax.rem(jnp.where(by_row, s, s // 2), 2)
        return rs, hr, cs, hc

    def score(s, slot):
        rs, hr, cs, hc = place(s)
        rows, cols = rows_of(rs * 4 + hr * 2, 2), rows_of(cs * 4 + hc * 2, 2)
        eh, ch = e_hi[rows, :], c_hi[cols, :]
        scores_v[slot] = lax.dot_general(
            jnp.concatenate([eh, eh, e_lo[rows, :]], axis=1),
            jnp.concatenate([ch, c_lo[cols, :], ch], axis=1),
            (((1,), (1,)), ((), ())),
            preferred_element_type=jnp.float32,
        )

    def work(s, slot):
        score(jnp.minimum(s + 1, 15), 1 - slot)
        rs, hr, cs, hc = place(s)
        zr, zc = jnp.where(rs == 0, blocks[0], blocks[1]), lax.rem(zh + cs, 2)
        first_row, first_col = rs * 4 + hr * 2, cs * 4 + hc * 2
        rows, cols = rows_of(first_row, 2), rows_of(first_col, 2)
        count_rows = [
            pl.ds(
                pl.multiple_of((zr * 4 + piece_y(ring(x, k), h)) * share + h * half, half), half
            )
            for k in (1 + hr, 3 - 3 * hr)
            for h in range(2)
        ]
        count_cols = [rows_of(zc * 4 + ring(y, k)) for k in (1 + hc, 3 - 3 * hc)]
        counts = jnp.concatenate(
            [jnp.concatenate([cooc_v[r, c] for c in count_cols], axis=1) for r in count_rows],
            axis=0,
        )
        logs_row = jnp.concatenate([row_log[rows, :]] * (2 * share // 128), axis=1)
        logs_col = jnp.concatenate([col_log[first_col + k, :1, :] for k in range(2)], axis=1)
        centred = scores_v[slot] + logs_row + logs_col
        counts_f = jnp.maximum(counts.astype(jnp.float32), 1.0)
        slopes = listed(zr * 2 + zc) * jnp.where(
            counts > 0,
            (0.1 + 0.25 * (counts_f * lax.rsqrt(counts_f))) * (centred - jnp.log(counts_f)),
            1.0 / (1.0 + jnp.exp(-centred)),
        )
        sh, sl = split(slopes)
        ch = c_hi[cols, :]
        to_rows = jnp.dot(
            jnp.concatenate([sh, sh, sl], axis=1),
            jnp.concatenate([ch, c_lo[cols, :], ch], axis=0),
            preferred_element_type=jnp.float32,
        )
        for k in range(2):
            for h in range(2):
                start_at = k * share + h * half
                row_grad[h, rs, hr * 2 + k] += to_rows[start_at : start_at + half]
        th = jnp.concatenate([et_hi[first_row + k] for k in range(2)], axis=1)
        tl = jnp.concatenate([et_lo[first_row + k] for k in range(2)], axis=1)
        to_cols = jnp.dot(
            jnp.concatenate([th, tl, th], axis=1),
            jnp.concatenate([sh, sh, sl], axis=0),
            preferred_element_type=jnp.float32,
        )
        for k in range(2):
            col_grad[cs, hc * 2 + k] += to_cols[:, k * share : (k + 1) * share]

    def before1():
        arrive(sib_pieces[2:])
        convert_rows(0, 2, 4)

    def before3():
        arrive(col_out[1])
        convert_cols(1, 0, 2)

    def before4():
        col_far.wait_recv()
        convert_cols(1, 2, 4)

    def before5():
        arrive(row_out[1])
        sib_block.start()

    def before7():
        sib_block.wait_recv()
        convert_rows(1, 0, 4)

    def before8():
        sib_back[0].start()

    def before9():
        sib_back[0].wait_recv()
        row_grad[q, 0] += sib_in[0]
        start(row_back[0])

    def before10():
        start(col_back[1])

    def before12():
        far_back.start()

    def before14():
        sib_back[1].start()
        arrive(row_back[0])
        row_grad[q, 0, 3] += (row_in[0, 0] + row_in[0, 1]) + row_in[0, 2]

        @pl.when(relay_self)
        def _():
            feed_here.start()

        @pl.when(jnp.logical_not(relay_self))
        def _():
            feed[0].start()

    def before15():
        start(col_back[0][:2])
        sib_back[1].wait_recv()
        row_grad[q, 1, pl.ds(0, 2)] += sib_in[1, pl.ds(0, 2)]
        start(row_back[1][:2])
        arrive(col_back[1])
        col_grad[1, 3] += col_in[1, 0] + col_in[1, 1]
        pair_back.start()

    events = {
        1: before1,
        3: before3,
        4: before4,
        5: before5,
        7: before7,
        8: before8,
        9: before9,
        10: before10,
        12: before12,
        14: before14,
        15: before15,
    }

    score(0, 0)

    def pair(i, carry):
        for u in range(2):
            for s, event in events.items():
                if s % 2 == u:
                    pl.when(i == s // 2)(event)
            work(2 * i + u, u)
        return carry

    lax.fori_loop(0, 8, pair, 0)

    sib_back[2].start()
    far_back.wait_recv()
    col_grad[0, 2] += col_in[1, 2]
    col_back[0][2].start()
    sib_back[2].wait_recv()
    row_grad[q, 1, pl.ds(2, 2)] += sib_in[1, pl.ds(2, 2)]
    row_back[1][2].start()
    arrive(row_back[1])
    row_grad[q, 1, 3] += (row_in[1, 0] + row_in[1, 1]) + row_in[1, 2]
    feed[1].start()
    for s in range(2):
        slot = row_feed.at[s]
        pltpu.make_async_copy(slot, slot, recv_sems.at[feed_sem + s]).wait()
    row_feed[0] += row_feed[1]

    @pl.when(jnp.logical_not(ends_here))
    def _():
        home.start()

    arrive(col_back[0])
    col_grad[0, 3] += (col_in[0, 0] + col_in[0, 1]) + col_in[0, 2]
    pair_back.wait_recv()
    grad_ref[...] = (col_grad[0, 3] + col_last[...]).T

    @pl.when(is_owner)
    def _():
        for k in range(2):
            part = pl.ds(k * half, half)

            @pl.when(x_place[k] == x)
            def _():
                grad_ref[part, :] += row_feed[0]

            @pl.when(x_place[k] != x)
            def _():
                slot = row_home.at[k]
                pltpu.make_async_copy(slot, slot, recv_sems.at[home_sem + k]).wait()
                grad_ref[part, :] += row_home[k]

        for copy in scatter:
            copy.wait_send()

    @pl.when(jnp.logical_not(relay_self))
    def _():
        feed[0].wait_send()

    feed[1].wait_send()

    @pl.when(jnp.logical_not(ends_here))
    def _():
        home.wait_send()

    net.finish()


def local(cooc, tile_list, marginal, embed, accum):
    share, width = embed.shape
    half = share // 2
    items = 8 * share
    f32, bf16 = jnp.float32, jnp.bfloat16
    hbm = pl.BlockSpec(memory_space=pl.ANY)
    vmem = pl.BlockSpec(memory_space=pltpu.VMEM)
    smem = pl.BlockSpec(memory_space=pltpu.SMEM)
    summed = pl.pallas_call(
        kernel,
        out_shape=jax.ShapeDtypeStruct((share, width), f32),
        in_specs=[hbm, vmem, smem, hbm],
        out_specs=vmem,
        scratch_shapes=[
            pltpu.VMEM((2, 4, share + PAD, width), f32),
            pltpu.VMEM((2, 2, 4, half + PAD, width), f32),
            pltpu.VMEM((2, half + PAD, width), f32),
            pltpu.VMEM((items, items), jnp.int32),
            pltpu.VMEM((items, width), bf16),
            pltpu.VMEM((items, width), bf16),
            pltpu.VMEM((8, width, share), bf16),
            pltpu.VMEM((8, width, share), bf16),
            pltpu.VMEM((items, width), bf16),
            pltpu.VMEM((items, width), bf16),
            pltpu.VMEM((items, 128), f32),
            pltpu.VMEM((8, PAD, share), f32),
            pltpu.VMEM((2, 2 * share, 2 * share), f32),
            pltpu.VMEM((2, 2, 4, half, width), f32),
            pltpu.VMEM((2, 4, width, share), f32),
            pltpu.VMEM((2, 4, half, width), f32),
            pltpu.VMEM((2, 3, half, width), f32),
            pltpu.VMEM((2, half, width), f32),
            pltpu.VMEM((2, half, width), f32),
            pltpu.VMEM((2, 3, width, share), f32),
            pltpu.VMEM((width, share), f32),
            pltpu.VMEM((8, 8, 128), f32),
            pltpu.VMEM((4, 8, 128), f32),
            pltpu.VMEM((4, 8, 128), f32),
            pltpu.SemaphoreType.DMA((N_SEND,)),
            pltpu.SemaphoreType.DMA((N_RECV,)),
            pltpu.SemaphoreType.DMA((9,)),
        ],
        compiler_params=pltpu.CompilerParams(
            collective_id=0, has_side_effects=True, vmem_limit_bytes=56 * 2**20
        ),
        cost_estimate=pl.CostEstimate(
            flops=18 * items * items * width, bytes_accessed=4 * items * items, transcendentals=0
        ),
    )(embed, marginal.reshape(1, share), tile_list.reshape(1, 4), cooc)
    gradients = summed / (items // 2)
    new_accum = accum + gradients * gradients
    new_embed = embed - LEARN_RATE * gradients / jnp.sqrt(new_accum)
    return (new_embed, new_accum)


def solution(mesh):
    placed = (
        P("row", "col"),
        P("row", "col", None),
        P(("col", "row")),
        P(("col", "row"), None),
        P(("col", "row"), None),
    )
    return jax.shard_map(
        local,
        mesh=mesh,
        in_specs=placed,
        out_specs=(P(("col", "row"), None), P(("col", "row"), None)),
        check_vma=False,
    )
```

```python
import jax
import jax.numpy as jnp
from jax import lax
from jax.experimental import pallas as pl
from jax.experimental.pallas import tpu as pltpu
from jax.sharding import PartitionSpec as P

LEARN_RATE = 0.05
MESH = pl.DeviceIdType.MESH
PAD = 8
RING = 4
N_SEND = 64
N_RECV = 48


def split(value):
    high = value.astype(jnp.bfloat16)
    low = (value - high.astype(jnp.float32)).astype(jnp.bfloat16)
    return high, low


class Copies:
    def __init__(self, send_sems, recv_sems):
        self.send_sems, self.recv_sems = send_sems, recv_sems
        self.sends = self.recvs = 0
        self.pending = []

    def send_sem(self):
        self.sends += 1
        return self.send_sems.at[self.sends - 1]

    def recv_sem(self, count=1):
        self.recvs += count
        return self.recvs - count

    def make(self, src, dst, device):
        copy = pltpu.make_async_remote_copy(
            src_ref=src,
            dst_ref=dst,
            send_sem=self.send_sem(),
            recv_sem=self.recv_sems.at[self.recv_sem()],
            device_id=device,
            device_id_type=MESH,
        )
        self.pending.append(copy)
        return copy

    def finish(self):
        for copy in self.pending:
            copy.wait_send()


def kernel(
    embed_hbm,
    marg_hbm,
    tiles_hbm,
    cooc_hbm,
    grad_ref,
    col_land,
    row_land,
    row_src,
    cooc_v,
    e_hi,
    e_lo,
    et_hi,
    et_lo,
    c_hi,
    c_lo,
    row_log,
    col_log,
    scores_v,
    row_grad,
    col_grad,
    sib_in,
    row_in,
    row_feed,
    row_home,
    col_in,
    col_last,
    marg_ref,
    tiles_ref,
    tot1,
    tot2,
    tot3,
    send_sems,
    recv_sems,
    local_sems,
):
    share, width = embed_hbm.shape
    half = share // 2
    row = lax.axis_index("row")
    col = lax.axis_index("col")
    zh, y = row // 4, lax.rem(row, 4)
    x, zl, q = col // 4, lax.rem(col // 2, 2), lax.rem(col, 2)

    def device(zh_=zh, y_=y, x_=x, zl_=zl, q_=q):
        return (zh_ * 4 + y_, x_ * 4 + zl_ * 2 + q_)

    def ring(position, step):
        return lax.rem(position + step + RING, RING)

    def offset(o):
        return jnp.where(o == 0, 1, jnp.where(o == 1, 3, jnp.where(o == 2, 2, 0)))

    is_owner = col < 8

    def flip(bit, by):
        return 1 - bit if by else bit

    near = [
        device(zh_=flip(zh, k // 4), zl_=flip(zl, k // 2 % 2), q_=flip(q, k % 2))
        for k in range(1, 8)
    ]
    near_y = [device(y_=ring(y, k)) for k in range(1, 4)]
    near_x = [device(x_=ring(x, k)) for k in range(1, 4)]
    by_y = [near_y[0], near_y[2], near_y[1]]
    by_x = [near_x[0], near_x[2], near_x[1]]
    sibling, zl_pair, zh_pair = near[0], near[1], near[3]
    blocks = [lax.rem(zh + zl + s + y // 2, 2) for s in range(2)]

    def piece_y(x_, h):
        return lax.rem(zh + 1 + 2 * h + y - x_ + RING, RING)

    source = [(blocks[s] * 4 + piece_y(x, q), row) for s in range(2)]
    relay_self = jnp.logical_and(source[0][0] == row, x * 4 + y == col)
    x_place = [lax.rem(x + 1 + 2 * k - y + zl * 2 + q + RING, RING) for k in range(2)]
    zl_place = lax.rem(zl + zh + x, 2)
    targets = [(col, x_place[k] * 4 + zl_place * 2 + k) for k in range(2)]
    relay = [(source[s][0], x * 4 + y) for s in range(2)]
    relay_y = zl * 2 + q
    turn = lax.rem(x + 3 + y - relay_y + RING, RING)
    back_zh, back_h = lax.rem(turn, 2), turn // 2
    back_zl = lax.rem(zl + zh + back_zh, 2)
    feeders = [
        (back_zh * 4 + relay_y, x * 4 + lax.rem(back_zl + s, 2) * 2 + back_h) for s in range(2)
    ]
    feeds_self = jnp.logical_and(feeders[0][0] == row, feeders[0][1] == col)

    def signal(other):
        pl.semaphore_signal(barrier, inc=1, device_id=other, device_id_type=MESH)

    barrier = pltpu.get_barrier_semaphore()
    for other in near + near_y + near_x + [source[0], feeders[1]]:
        signal(other)

    @pl.when(jnp.logical_not(feeds_self))
    def _():
        signal(feeders[0])

    embed_in = pltpu.make_async_copy(
        embed_hbm, col_land.at[zh, y, pl.ds(0, share)], local_sems.at[0]
    )
    embed_in.start()
    marg_in = pltpu.make_async_copy(marg_hbm, marg_ref, local_sems.at[9])
    marg_in.start()
    tiles_in = pltpu.make_async_copy(tiles_hbm, tiles_ref, local_sems.at[10])
    tiles_in.start()
    cooc_in = [
        pltpu.make_async_copy(
            cooc_hbm.at[pl.ds(p * share, share)],
            cooc_v.at[pl.ds(p * share, share)],
            local_sems.at[1 + p],
        )
        for p in range(8)
    ]

    for copy in cooc_in:
        copy.start()

    marg_in.wait()
    marg = marg_ref[...].astype(jnp.float32)
    logs = jnp.log(marg)
    tot1[0] = jnp.broadcast_to(jnp.sum(marg, axis=1, keepdims=True), tot1.shape[1:])
    embed_in.wait()
    col_land[zh, y, pl.ds(share, PAD), :] = jnp.broadcast_to(logs, (PAD, width))
    for h in range(2):
        row_src[h, pl.ds(0, half), :] = col_land[zh, y, pl.ds(h * half, half), :]
        row_src[h, pl.ds(half, PAD), :] = jnp.broadcast_to(
            jnp.concatenate([logs[:, h * half : (h + 1) * half]] * 2, axis=1), (PAD, width)
        )

    pl.semaphore_wait(barrier, 14 + jnp.where(relay_self, 0, 1) + jnp.where(is_owner, 2, 0))

    net = Copies(send_sems, recv_sems)

    def spread(block_ref, others):
        sem = recv_sems.at[net.recv_sem()]
        for k, other in enumerate(others):
            copy = pltpu.make_async_remote_copy(
                src_ref=block_ref.at[0],
                dst_ref=block_ref.at[k + 1],
                send_sem=net.send_sem(),
                recv_sem=sem,
                device_id=other,
                device_id_type=MESH,
            )
            copy.start()
            net.pending.append(copy)
        landed = block_ref.at[pl.ds(1, len(others))]
        return pltpu.make_async_copy(landed, landed, sem)

    def same(ref, other):
        return net.make(ref, ref, other)

    def start(copies):
        for copy in copies:
            copy.start()

    def arrive(copies):
        for copy in copies:
            copy.wait_recv()

    zls, zhs = (zl, 1 - zl), (zh, 1 - zh)
    scatter_recv = recv_sems.at[net.recv_sem()]
    scatter = [
        pltpu.make_async_remote_copy(
            src_ref=row_src.at[k],
            dst_ref=row_land.at[zl_place, k, x_place[k]],
            send_sem=net.send_sem(),
            recv_sem=scatter_recv,
            device_id=targets[k],
            device_id_type=MESH,
        )
        for k in range(2)
    ]
    col_pair = same(col_land.at[zh, y], zh_pair)
    row_pair = same(row_land.at[zl, q, x], zl_pair)
    col_out = [[same(col_land.at[zhs[s], y], other) for other in by_y[:2]] for s in range(2)]
    upper, lower = pl.ds(0, half + PAD), pl.ds(half + PAD, half)
    col_relay = [
        same(col_land.at[zh, ring(y, -1), upper], by_y[0]),
        same(col_land.at[zh, ring(y, 1), lower], by_y[1]),
    ]
    col_far = same(col_land.at[zh, ring(y, 2)], zh_pair)
    row_out = [[same(row_land.at[zls[s], q, x], other) for other in by_x] for s in range(2)]
    sib_pieces = [same(row_land.at[zl, q, ring(x, step)], sibling) for step in (1, 3, 2, 0)]
    sib_block = same(row_land.at[1 - zl, q], sibling)
    sib_parts = [(0, 0, 4), (1, 0, 2), (1, 2, 2)]
    sib_back = [
        net.make(row_grad.at[1 - q, s, pl.ds(a, n)], sib_in.at[s, pl.ds(a, n)], sibling)
        for s, a, n in sib_parts
    ]
    col_back = [
        [net.make(col_grad.at[0, o], col_in.at[0, o], by_y[o]) for o in range(3)],
        [net.make(col_grad.at[1, o], col_in.at[1, o], by_y[o]) for o in range(2)],
    ]
    far_back = net.make(col_grad.at[1, 2], col_in.at[1, 2], zh_pair)
    row_back = [
        [net.make(row_grad.at[q, s, o], row_in.at[s, o], by_x[o]) for o in range(3)]
        for s in range(2)
    ]
    pair_back = net.make(col_grad.at[1, 3], col_last, zh_pair)
    feed_sem = net.recv_sem(2)
    feed = [
        pltpu.make_async_remote_copy(
            src_ref=row_grad.at[q, s, 3],
            dst_ref=row_feed.at[s],
            send_sem=net.send_sem(),
            recv_sem=recv_sems.at[feed_sem + s],
            device_id=relay[s],
            device_id_type=MESH,
        )
        for s in range(2)
    ]
    feed_here = pltpu.make_async_copy(
        row_grad.at[q, 0, 3], row_feed.at[0], recv_sems.at[feed_sem]
    )
    home_sem = net.recv_sem(2)
    home = pltpu.make_async_remote_copy(
        src_ref=row_feed.at[0],
        dst_ref=row_home.at[back_h],
        send_sem=net.send_sem(),
        recv_sem=recv_sems.at[home_sem + back_h],
        device_id=device(x_=back_zh),
        device_id_type=MESH,
    )
    ends_here = x == back_zh

    @pl.when(is_owner)
    def _():
        start(scatter)

    start(col_out[0])
    stage1 = spread(tot1, near)
    row_grad[...] = jnp.zeros_like(row_grad)
    col_grad[...] = jnp.zeros_like(col_grad)
    stage1.wait()
    tot2[0] = jnp.sum(tot1[...], axis=0)
    stage2 = spread(tot2, near_x)
    scatter[0].wait_recv()
    start([*row_out[0][:2], sib_pieces[3], row_out[0][2], col_pair, row_pair])
    stage2.wait()
    tot3[0] = jnp.sum(tot2[...], axis=0)
    stage3 = spread(tot3, near_y)
    col_out[0][0].wait_recv()
    col_relay[0].start()
    col_out[0][1].wait_recv()
    col_relay[1].start()
    for k in range(2):
        row_out[0][k].wait_recv()
        sib_pieces[1 - k].start()
    stage3.wait()
    log_total = jnp.log(jnp.sum(tot3[...], axis=0))[:1, :1]

    def rows_of(index, count=1):
        return pl.ds(pl.multiple_of(index * share, share), count * share)

    def convert_cols(s, first, last):
        def piece(o, carry):
            at = ring(y, offset(o))
            index = s * 4 + o
            rows = rows_of(index)
            c_hi[rows, :], c_lo[rows, :] = split(col_land[zhs[s], at, pl.ds(0, share), :])
            col_log[index] = col_land[zhs[s], at, pl.ds(share, PAD), :] - log_total
            return carry

        lax.fori_loop(first, last, piece, 0)

    def convert_rows(s, first, last):
        def piece(o, carry):
            at = ring(x, offset(o))
            index = s * 4 + o
            rows = rows_of(index)
            values = jnp.concatenate(
                [row_land[zls[s], h, at, pl.ds(0, half), :] for h in range(2)], axis=0
            )
            e_hi[rows, :], e_lo[rows, :] = split(values)
            et_hi[index], et_lo[index] = split(values.T)
            for h in range(2):
                line = row_land[zls[s], h, at, pl.ds(half, 1), pl.ds(0, half)]
                row_log[
                    pl.ds(pl.multiple_of(index * share + h * half, half), half), :
                ] = jnp.broadcast_to(line, (128, half)).T
            return carry

        lax.fori_loop(first, last, piece, 0)

    col_pair.wait_recv()
    start(col_out[1])
    arrive(col_relay)
    col_far.start()
    convert_cols(0, 0, 4)
    arrive(sib_pieces[:2])
    convert_rows(0, 0, 2)
    row_out[0][2].wait_recv()
    sib_pieces[2].start()
    row_pair.wait_recv()
    start(row_out[1])
    for copy in cooc_in:
        copy.wait()

    tiles_in.wait()
    entries = [tiles_ref[0, k] for k in range(4)]

    def listed(t):
        on = [jnp.where(entry == t, jnp.float32(1), jnp.float32(0)) for entry in entries]
        return (on[0] + on[1]) + (on[2] + on[3])

    def place(s):
        rs = s // 8
        cs = jnp.where(jnp.logical_and(s >= 4, s < 12), 1, 0)
        by_row = jnp.logical_or(s < 4, s >= 12)
        hr = lax.rem(jnp.where(by_row, s // 2, s), 2)
        hc = lax.rem(jnp.where(by_row, s, s // 2), 2)
        return rs, hr, cs, hc

    def score(s, slot):
        rs, hr, cs, hc = place(s)
        rows, cols = rows_of(rs * 4 + hr * 2, 2), rows_of(cs * 4 + hc * 2, 2)
        eh, ch = e_hi[rows, :], c_hi[cols, :]
        scores_v[slot] = lax.dot_general(
            jnp.concatenate([eh, eh, e_lo[rows, :]], axis=1),
            jnp.concatenate([ch, c_lo[cols, :], ch], axis=1),
            (((1,), (1,)), ((), ())),
            preferred_element_type=jnp.float32,
        )

    def work(s, slot):
        score(jnp.minimum(s + 1, 15), 1 - slot)
        rs, hr, cs, hc = place(s)
        zr, zc = jnp.where(rs == 0, blocks[0], blocks[1]), lax.rem(zh + cs, 2)
        first_row, first_col = rs * 4 + hr * 2, cs * 4 + hc * 2
        rows, cols = rows_of(first_row, 2), rows_of(first_col, 2)
        count_rows = [
            pl.ds(
                pl.multiple_of((zr * 4 + piece_y(ring(x, k), h)) * share + h * half, half), half
            )
            for k in (1 + hr, 3 - 3 * hr)
            for h in range(2)
        ]
        count_cols = [rows_of(zc * 4 + ring(y, k)) for k in (1 + hc, 3 - 3 * hc)]
        counts = jnp.concatenate(
            [jnp.concatenate([cooc_v[r, c] for c in count_cols], axis=1) for r in count_rows],
            axis=0,
        )
        logs_row = jnp.concatenate([row_log[rows, :]] * (2 * share // 128), axis=1)
        logs_col = jnp.concatenate([col_log[first_col + k, :1, :] for k in range(2)], axis=1)
        centred = scores_v[slot] + logs_row + logs_col
        counts_f = jnp.maximum(counts.astype(jnp.float32), 1.0)
        slopes = listed(zr * 2 + zc) * jnp.where(
            counts > 0,
            (0.1 + 0.25 * (counts_f * lax.rsqrt(counts_f))) * (centred - jnp.log(counts_f)),
            1.0 / (1.0 + jnp.exp(-centred)),
        )
        sh, sl = split(slopes)
        ch = c_hi[cols, :]
        to_rows = jnp.dot(
            jnp.concatenate([sh, sh, sl], axis=1),
            jnp.concatenate([ch, c_lo[cols, :], ch], axis=0),
            preferred_element_type=jnp.float32,
        )
        for k in range(2):
            for h in range(2):
                start_at = k * share + h * half
                row_grad[h, rs, hr * 2 + k] += to_rows[start_at : start_at + half]
        th = jnp.concatenate([et_hi[first_row + k] for k in range(2)], axis=1)
        tl = jnp.concatenate([et_lo[first_row + k] for k in range(2)], axis=1)
        to_cols = jnp.dot(
            jnp.concatenate([th, tl, th], axis=1),
            jnp.concatenate([sh, sh, sl], axis=0),
            preferred_element_type=jnp.float32,
        )
        for k in range(2):
            col_grad[cs, hc * 2 + k] += to_cols[:, k * share : (k + 1) * share]

    def before1():
        arrive(sib_pieces[2:])
        convert_rows(0, 2, 4)

    def before3():
        arrive(col_out[1])
        convert_cols(1, 0, 2)

    def before5():
        arrive(row_out[1])
        sib_block.start()
        col_far.wait_recv()
        convert_cols(1, 2, 4)

    def before7():
        sib_block.wait_recv()
        convert_rows(1, 0, 4)

    def before8():
        sib_back[0].start()

    def before9():
        sib_back[0].wait_recv()
        row_grad[q, 0] += sib_in[0]
        start(row_back[0])

    def before10():
        start(col_back[1])

    def before12():
        far_back.start()

    def before14():
        sib_back[1].start()
        arrive(row_back[0])
        row_grad[q, 0, 3] += (row_in[0, 0] + row_in[0, 1]) + row_in[0, 2]

        @pl.when(relay_self)
        def _():
            feed_here.start()

        @pl.when(jnp.logical_not(relay_self))
        def _():
            feed[0].start()

    def before15():
        start(col_back[0][:2])
        sib_back[1].wait_recv()
        row_grad[q, 1, pl.ds(0, 2)] += sib_in[1, pl.ds(0, 2)]
        start(row_back[1][:2])
        arrive(col_back[1])
        col_grad[1, 3] += col_in[1, 0] + col_in[1, 1]
        pair_back.start()

    events = {
        1: before1,
        3: before3,
        5: before5,
        7: before7,
        8: before8,
        9: before9,
        10: before10,
        12: before12,
        14: before14,
        15: before15,
    }

    score(0, 0)

    def pair(i, carry):
        for u in range(2):
            for s, event in events.items():
                if s % 2 == u:
                    pl.when(i == s // 2)(event)
            work(2 * i + u, u)
        return carry

    lax.fori_loop(0, 8, pair, 0)

    sib_back[2].start()
    far_back.wait_recv()
    col_grad[0, 2] += col_in[1, 2]
    col_back[0][2].start()
    sib_back[2].wait_recv()
    row_grad[q, 1, pl.ds(2, 2)] += sib_in[1, pl.ds(2, 2)]
    row_back[1][2].start()
    arrive(row_back[1])
    row_grad[q, 1, 3] += (row_in[1, 0] + row_in[1, 1]) + row_in[1, 2]
    feed[1].start()
    for s in range(2):
        slot = row_feed.at[s]
        pltpu.make_async_copy(slot, slot, recv_sems.at[feed_sem + s]).wait()
    row_feed[0] += row_feed[1]

    @pl.when(jnp.logical_not(ends_here))
    def _():
        home.start()

    arrive(col_back[0])
    col_grad[0, 3] += (col_in[0, 0] + col_in[0, 1]) + col_in[0, 2]
    pair_back.wait_recv()
    grad_ref[...] = (col_grad[0, 3] + col_last[...]).T

    @pl.when(is_owner)
    def _():
        for k in range(2):
            part = pl.ds(k * half, half)

            @pl.when(x_place[k] == x)
            def _():
                grad_ref[part, :] += row_feed[0]

            @pl.when(x_place[k] != x)
            def _():
                slot = row_home.at[k]
                pltpu.make_async_copy(slot, slot, recv_sems.at[home_sem + k]).wait()
                grad_ref[part, :] += row_home[k]

        for copy in scatter:
            copy.wait_send()

    @pl.when(jnp.logical_not(relay_self))
    def _():
        feed[0].wait_send()

    feed[1].wait_send()

    @pl.when(jnp.logical_not(ends_here))
    def _():
        home.wait_send()

    net.finish()


def local(cooc, tile_list, marginal, embed, accum):
    share, width = embed.shape
    half = share // 2
    items = 8 * share
    f32, bf16 = jnp.float32, jnp.bfloat16
    hbm = pl.BlockSpec(memory_space=pl.ANY)
    vmem = pl.BlockSpec(memory_space=pltpu.VMEM)
    summed = pl.pallas_call(
        kernel,
        out_shape=jax.ShapeDtypeStruct((share, width), f32),
        in_specs=[hbm, hbm, hbm, hbm],
        out_specs=vmem,
        scratch_shapes=[
            pltpu.VMEM((2, 4, share + PAD, width), f32),
            pltpu.VMEM((2, 2, 4, half + PAD, width), f32),
            pltpu.VMEM((2, half + PAD, width), f32),
            pltpu.VMEM((items, items), jnp.int32),
            pltpu.VMEM((items, width), bf16),
            pltpu.VMEM((items, width), bf16),
            pltpu.VMEM((8, width, share), bf16),
            pltpu.VMEM((8, width, share), bf16),
            pltpu.VMEM((items, width), bf16),
            pltpu.VMEM((items, width), bf16),
            pltpu.VMEM((items, 128), f32),
            pltpu.VMEM((8, PAD, share), f32),
            pltpu.VMEM((2, 2 * share, 2 * share), f32),
            pltpu.VMEM((2, 2, 4, half, width), f32),
            pltpu.VMEM((2, 4, width, share), f32),
            pltpu.VMEM((2, 4, half, width), f32),
            pltpu.VMEM((2, 3, half, width), f32),
            pltpu.VMEM((2, half, width), f32),
            pltpu.VMEM((2, half, width), f32),
            pltpu.VMEM((2, 3, width, share), f32),
            pltpu.VMEM((width, share), f32),
            pltpu.VMEM((1, share), jnp.int32),
            pltpu.SMEM((1, 4), jnp.int32),
            pltpu.VMEM((8, 8, 128), f32),
            pltpu.VMEM((4, 8, 128), f32),
            pltpu.VMEM((4, 8, 128), f32),
            pltpu.SemaphoreType.DMA((N_SEND,)),
            pltpu.SemaphoreType.DMA((N_RECV,)),
            pltpu.SemaphoreType.DMA((11,)),
        ],
        compiler_params=pltpu.CompilerParams(
            collective_id=0, has_side_effects=True, vmem_limit_bytes=56 * 2**20
        ),
        cost_estimate=pl.CostEstimate(
            flops=18 * items * items * width, bytes_accessed=4 * items * items, transcendentals=0
        ),
    )(embed, marginal.reshape(1, share), tile_list.reshape(1, 4), cooc)
    gradients = summed / (items // 2)
    new_accum = accum + gradients * gradients
    new_embed = embed - LEARN_RATE * gradients / jnp.sqrt(new_accum)
    return (new_embed, new_accum)


def solution(mesh):
    placed = (
        P("row", "col"),
        P("row", "col", None),
        P(("col", "row")),
        P(("col", "row"), None),
        P(("col", "row"), None),
    )
    return jax.shard_map(
        local,
        mesh=mesh,
        in_specs=placed,
        out_specs=(P(("col", "row"), None), P(("col", "row"), None)),
        check_vma=False,
    )
```

```python
import jax
import jax.numpy as jnp
from jax import lax
from jax.experimental import pallas as pl
from jax.experimental.pallas import tpu as pltpu
from jax.sharding import PartitionSpec as P

LEARN_RATE = 0.05
MESH = pl.DeviceIdType.MESH
PAD = 8
RING = 4
N_SEND = 64
N_RECV = 48


def split(value):
    high = value.astype(jnp.bfloat16)
    low = (value - high.astype(jnp.float32)).astype(jnp.bfloat16)
    return high, low


class Copies:
    def __init__(self, send_sems, recv_sems):
        self.send_sems, self.recv_sems = send_sems, recv_sems
        self.sends = self.recvs = 0
        self.pending = []

    def send_sem(self):
        self.sends += 1
        return self.send_sems.at[self.sends - 1]

    def recv_sem(self, count=1):
        self.recvs += count
        return self.recvs - count

    def make(self, src, dst, device):
        copy = pltpu.make_async_remote_copy(
            src_ref=src,
            dst_ref=dst,
            send_sem=self.send_sem(),
            recv_sem=self.recv_sems.at[self.recv_sem()],
            device_id=device,
            device_id_type=MESH,
        )
        self.pending.append(copy)
        return copy

    def finish(self):
        for copy in self.pending:
            copy.wait_send()


def kernel(
    embed_hbm,
    marg_hbm,
    tiles_hbm,
    cooc_hbm,
    grad_ref,
    col_land,
    row_land,
    row_src,
    cooc_v,
    e_hi,
    e_lo,
    et_hi,
    et_lo,
    c_hi,
    c_lo,
    row_log,
    col_log,
    scores_v,
    row_grad,
    col_grad,
    sib_in,
    row_in,
    row_feed,
    row_home,
    col_in,
    col_last,
    marg_ref,
    tiles_ref,
    tot1,
    tot2,
    tot3,
    send_sems,
    recv_sems,
    local_sems,
):
    share, width = embed_hbm.shape
    half = share // 2
    row = lax.axis_index("row")
    col = lax.axis_index("col")
    zh, y = row // 4, lax.rem(row, 4)
    x, zl, q = col // 4, lax.rem(col // 2, 2), lax.rem(col, 2)

    def device(zh_=zh, y_=y, x_=x, zl_=zl, q_=q):
        return (zh_ * 4 + y_, x_ * 4 + zl_ * 2 + q_)

    def ring(position, step):
        return lax.rem(position + step + RING, RING)

    def offset(o):
        return jnp.where(o == 0, 1, jnp.where(o == 1, 3, jnp.where(o == 2, 2, 0)))

    is_owner = col < 8

    def flip(bit, by):
        return 1 - bit if by else bit

    near = [
        device(zh_=flip(zh, k // 4), zl_=flip(zl, k // 2 % 2), q_=flip(q, k % 2))
        for k in range(1, 8)
    ]
    near_y = [device(y_=ring(y, k)) for k in range(1, 4)]
    near_x = [device(x_=ring(x, k)) for k in range(1, 4)]
    by_y = [near_y[0], near_y[2], near_y[1]]
    by_x = [near_x[0], near_x[2], near_x[1]]
    sibling, zl_pair, zh_pair = near[0], near[1], near[3]
    blocks = [lax.rem(zh + zl + s + y // 2, 2) for s in range(2)]

    def piece_y(x_, h):
        return lax.rem(zh + 1 + 2 * h + y - x_ + RING, RING)

    source = [(blocks[s] * 4 + piece_y(x, q), row) for s in range(2)]
    relay_self = jnp.logical_and(source[0][0] == row, x * 4 + y == col)
    x_place = [lax.rem(x + 1 + 2 * k - y + zl * 2 + q + RING, RING) for k in range(2)]
    zl_place = lax.rem(zl + zh + x, 2)
    targets = [(col, x_place[k] * 4 + zl_place * 2 + k) for k in range(2)]
    relay = [(source[s][0], x * 4 + y) for s in range(2)]
    relay_y = zl * 2 + q
    turn = lax.rem(x + 3 + y - relay_y + RING, RING)
    back_zh, back_h = lax.rem(turn, 2), turn // 2
    back_zl = lax.rem(zl + zh + back_zh, 2)
    feeders = [
        (back_zh * 4 + relay_y, x * 4 + lax.rem(back_zl + s, 2) * 2 + back_h) for s in range(2)
    ]
    feeds_self = jnp.logical_and(feeders[0][0] == row, feeders[0][1] == col)

    def signal(other):
        pl.semaphore_signal(barrier, inc=1, device_id=other, device_id_type=MESH)

    barrier = pltpu.get_barrier_semaphore()
    for other in near + near_y + near_x + [source[0], feeders[1]]:
        signal(other)

    @pl.when(jnp.logical_not(feeds_self))
    def _():
        signal(feeders[0])

    embed_in = pltpu.make_async_copy(
        embed_hbm, col_land.at[zh, y, pl.ds(0, share)], local_sems.at[0]
    )
    embed_in.start()
    marg_in = pltpu.make_async_copy(marg_hbm, marg_ref, local_sems.at[9])
    marg_in.start()
    tiles_in = pltpu.make_async_copy(tiles_hbm, tiles_ref, local_sems.at[10])
    tiles_in.start()
    cooc_in = [
        pltpu.make_async_copy(
            cooc_hbm.at[pl.ds(p * share, share)],
            cooc_v.at[pl.ds(p * share, share)],
            local_sems.at[1 + p],
        )
        for p in range(8)
    ]

    for copy in cooc_in:
        copy.start()

    marg_in.wait()
    marg = marg_ref[...].astype(jnp.float32)
    logs = jnp.log(marg)
    tot1[0] = jnp.broadcast_to(jnp.sum(marg, axis=1, keepdims=True), tot1.shape[1:])
    embed_in.wait()
    col_land[zh, y, pl.ds(share, PAD), :] = jnp.broadcast_to(logs, (PAD, width))
    for h in range(2):
        row_src[h, pl.ds(0, half), :] = col_land[zh, y, pl.ds(h * half, half), :]
        row_src[h, pl.ds(half, PAD), :] = jnp.broadcast_to(
            jnp.concatenate([logs[:, h * half : (h + 1) * half]] * 2, axis=1), (PAD, width)
        )

    pl.semaphore_wait(barrier, 14 + jnp.where(relay_self, 0, 1) + jnp.where(is_owner, 2, 0))

    net = Copies(send_sems, recv_sems)

    def spread(block_ref, others):
        sem = recv_sems.at[net.recv_sem()]
        for k, other in enumerate(others):
            copy = pltpu.make_async_remote_copy(
                src_ref=block_ref.at[0],
                dst_ref=block_ref.at[k + 1],
                send_sem=net.send_sem(),
                recv_sem=sem,
                device_id=other,
                device_id_type=MESH,
            )
            copy.start()
            net.pending.append(copy)
        landed = block_ref.at[pl.ds(1, len(others))]
        return pltpu.make_async_copy(landed, landed, sem)

    def same(ref, other):
        return net.make(ref, ref, other)

    def start(copies):
        for copy in copies:
            copy.start()

    def arrive(copies):
        for copy in copies:
            copy.wait_recv()

    zls, zhs = (zl, 1 - zl), (zh, 1 - zh)
    scatter_recv = recv_sems.at[net.recv_sem()]
    scatter = [
        pltpu.make_async_remote_copy(
            src_ref=row_src.at[k],
            dst_ref=row_land.at[zl_place, k, x_place[k]],
            send_sem=net.send_sem(),
            recv_sem=scatter_recv,
            device_id=targets[k],
            device_id_type=MESH,
        )
        for k in range(2)
    ]
    col_pair = same(col_land.at[zh, y], zh_pair)
    row_pair = same(row_land.at[zl, q, x], zl_pair)
    col_out = [[same(col_land.at[zhs[s], y], other) for other in by_y[:2]] for s in range(2)]
    upper, lower = pl.ds(0, half + PAD), pl.ds(half + PAD, half)
    col_relay = [
        same(col_land.at[zh, ring(y, -1), upper], by_y[0]),
        same(col_land.at[zh, ring(y, 1), lower], by_y[1]),
    ]
    col_far = same(col_land.at[zh, ring(y, 2)], zh_pair)
    row_out = [[same(row_land.at[zls[s], q, x], other) for other in by_x] for s in range(2)]
    sib_pieces = [same(row_land.at[zl, q, ring(x, step)], sibling) for step in (1, 3, 2, 0)]
    sib_block = same(row_land.at[1 - zl, q], sibling)
    sib_parts = [(0, 0, 4), (1, 0, 2), (1, 2, 2)]
    sib_back = [
        net.make(row_grad.at[1 - q, s, pl.ds(a, n)], sib_in.at[s, pl.ds(a, n)], sibling)
        for s, a, n in sib_parts
    ]
    col_back = [
        [net.make(col_grad.at[0, o], col_in.at[0, o], by_y[o]) for o in range(3)],
        [net.make(col_grad.at[1, o], col_in.at[1, o], by_y[o]) for o in range(2)],
    ]
    far_back = net.make(col_grad.at[1, 2], col_in.at[1, 2], zh_pair)
    row_back = [
        [net.make(row_grad.at[q, s, o], row_in.at[s, o], by_x[o]) for o in range(3)]
        for s in range(2)
    ]
    pair_back = net.make(col_grad.at[1, 3], col_last, zh_pair)
    feed_sem = net.recv_sem(2)
    feed = [
        pltpu.make_async_remote_copy(
            src_ref=row_grad.at[q, s, 3],
            dst_ref=row_feed.at[s],
            send_sem=net.send_sem(),
            recv_sem=recv_sems.at[feed_sem + s],
            device_id=relay[s],
            device_id_type=MESH,
        )
        for s in range(2)
    ]
    feed_here = pltpu.make_async_copy(
        row_grad.at[q, 0, 3], row_feed.at[0], recv_sems.at[feed_sem]
    )
    home_sem = net.recv_sem(2)
    home = pltpu.make_async_remote_copy(
        src_ref=row_feed.at[0],
        dst_ref=row_home.at[back_h],
        send_sem=net.send_sem(),
        recv_sem=recv_sems.at[home_sem + back_h],
        device_id=device(x_=back_zh),
        device_id_type=MESH,
    )
    ends_here = x == back_zh

    @pl.when(is_owner)
    def _():
        start(scatter)

    start(col_out[0])
    stage1 = spread(tot1, near)
    row_grad[...] = jnp.zeros_like(row_grad)
    col_grad[...] = jnp.zeros_like(col_grad)
    stage1.wait()
    tot2[0] = jnp.sum(tot1[...], axis=0)
    stage2 = spread(tot2, near_x)
    scatter[0].wait_recv()
    start([*row_out[0][:2], sib_pieces[3], row_out[0][2], col_pair, row_pair])
    stage2.wait()
    tot3[0] = jnp.sum(tot2[...], axis=0)
    stage3 = spread(tot3, near_y)
    col_out[0][0].wait_recv()
    col_relay[0].start()
    col_out[0][1].wait_recv()
    col_relay[1].start()
    for k in range(2):
        row_out[0][k].wait_recv()
        sib_pieces[1 - k].start()
    stage3.wait()
    log_total = jnp.log(jnp.sum(tot3[...], axis=0))[:1, :1]

    def rows_of(index, count=1):
        return pl.ds(pl.multiple_of(index * share, share), count * share)

    def convert_cols(s, first, last):
        def piece(o, carry):
            at = ring(y, offset(o))
            index = s * 4 + o
            rows = rows_of(index)
            c_hi[rows, :], c_lo[rows, :] = split(col_land[zhs[s], at, pl.ds(0, share), :])
            col_log[index] = col_land[zhs[s], at, pl.ds(share, PAD), :] - log_total
            return carry

        lax.fori_loop(first, last, piece, 0)

    def convert_rows(s, first, last):
        def piece(o, carry):
            at = ring(x, offset(o))
            index = s * 4 + o
            rows = rows_of(index)
            values = jnp.concatenate(
                [row_land[zls[s], h, at, pl.ds(0, half), :] for h in range(2)], axis=0
            )
            e_hi[rows, :], e_lo[rows, :] = split(values)
            et_hi[index], et_lo[index] = split(values.T)
            for h in range(2):
                line = row_land[zls[s], h, at, pl.ds(half, 1), pl.ds(0, half)]
                row_log[
                    pl.ds(pl.multiple_of(index * share + h * half, half), half), :
                ] = jnp.broadcast_to(line, (128, half)).T
            return carry

        lax.fori_loop(first, last, piece, 0)

    col_pair.wait_recv()
    start(col_out[1])
    arrive(col_relay)
    col_far.start()
    convert_cols(0, 0, 4)
    arrive(sib_pieces[:2])
    convert_rows(0, 0, 2)
    row_out[0][2].wait_recv()
    sib_pieces[2].start()
    row_pair.wait_recv()
    start(row_out[1])
    for copy in cooc_in:
        copy.wait()

    tiles_in.wait()
    entries = [tiles_ref[0, k] for k in range(4)]

    def listed(t):
        on = [jnp.where(entry == t, jnp.float32(1), jnp.float32(0)) for entry in entries]
        return (on[0] + on[1]) + (on[2] + on[3])

    def place(s):
        rs = s // 8
        cs = jnp.where(jnp.logical_and(s >= 4, s < 12), 1, 0)
        by_row = jnp.logical_or(s < 4, s >= 12)
        hr = lax.rem(jnp.where(by_row, s // 2, s), 2)
        hc = lax.rem(jnp.where(by_row, s, s // 2), 2)
        return rs, hr, cs, hc

    def score(s, slot):
        rs, hr, cs, hc = place(s)
        rows, cols = rows_of(rs * 4 + hr * 2, 2), rows_of(cs * 4 + hc * 2, 2)
        eh, ch = e_hi[rows, :], c_hi[cols, :]
        scores_v[slot] = lax.dot_general(
            jnp.concatenate([eh, eh, e_lo[rows, :]], axis=1),
            jnp.concatenate([ch, c_lo[cols, :], ch], axis=1),
            (((1,), (1,)), ((), ())),
            preferred_element_type=jnp.float32,
        )

    def work(s, slot, ahead=True):
        if ahead:
            score(s + 1, 1 - slot)
        rs, hr, cs, hc = place(s)
        zr, zc = jnp.where(rs == 0, blocks[0], blocks[1]), lax.rem(zh + cs, 2)
        first_row, first_col = rs * 4 + hr * 2, cs * 4 + hc * 2
        rows, cols = rows_of(first_row, 2), rows_of(first_col, 2)
        count_rows = [
            pl.ds(
                pl.multiple_of((zr * 4 + piece_y(ring(x, k), h)) * share + h * half, half), half
            )
            for k in (1 + hr, 3 - 3 * hr)
            for h in range(2)
        ]
        count_cols = [rows_of(zc * 4 + ring(y, k)) for k in (1 + hc, 3 - 3 * hc)]
        counts = jnp.concatenate(
            [jnp.concatenate([cooc_v[r, c] for c in count_cols], axis=1) for r in count_rows],
            axis=0,
        )
        logs_row = jnp.concatenate([row_log[rows, :]] * (2 * share // 128), axis=1)
        logs_col = jnp.concatenate([col_log[first_col + k, :1, :] for k in range(2)], axis=1)
        centred = scores_v[slot] + logs_row + logs_col
        counts_f = jnp.maximum(counts.astype(jnp.float32), 1.0)
        slopes = listed(zr * 2 + zc) * jnp.where(
            counts > 0,
            (0.1 + 0.25 * (counts_f * lax.rsqrt(counts_f))) * (centred - jnp.log(counts_f)),
            1.0 / (1.0 + jnp.exp(-centred)),
        )
        sh, sl = split(slopes)
        ch = c_hi[cols, :]
        to_rows = jnp.dot(
            jnp.concatenate([sh, sh, sl], axis=1),
            jnp.concatenate([ch, c_lo[cols, :], ch], axis=0),
            preferred_element_type=jnp.float32,
        )
        for k in range(2):
            for h in range(2):
                start_at = k * share + h * half
                row_grad[h, rs, hr * 2 + k] += to_rows[start_at : start_at + half]
        th = jnp.concatenate([et_hi[first_row + k] for k in range(2)], axis=1)
        tl = jnp.concatenate([et_lo[first_row + k] for k in range(2)], axis=1)
        to_cols = jnp.dot(
            jnp.concatenate([th, tl, th], axis=1),
            jnp.concatenate([sh, sh, sl], axis=0),
            preferred_element_type=jnp.float32,
        )
        for k in range(2):
            col_grad[cs, hc * 2 + k] += to_cols[:, k * share : (k + 1) * share]

    def before1():
        arrive(sib_pieces[2:])
        convert_rows(0, 2, 4)

    def before3():
        arrive(col_out[1])
        convert_cols(1, 0, 2)

    def before5():
        arrive(row_out[1])
        sib_block.start()
        col_far.wait_recv()
        convert_cols(1, 2, 4)

    def before7():
        sib_block.wait_recv()
        convert_rows(1, 0, 4)

    def before8():
        sib_back[0].start()

    def before9():
        sib_back[0].wait_recv()
        row_grad[q, 0] += sib_in[0]
        start(row_back[0])

    def before10():
        start(col_back[1])

    def before12():
        far_back.start()

    def before14():
        sib_back[1].start()
        arrive(row_back[0])
        row_grad[q, 0, 3] += (row_in[0, 0] + row_in[0, 1]) + row_in[0, 2]

        @pl.when(relay_self)
        def _():
            feed_here.start()

        @pl.when(jnp.logical_not(relay_self))
        def _():
            feed[0].start()

    def before15():
        start(col_back[0][:2])
        sib_back[1].wait_recv()
        row_grad[q, 1, pl.ds(0, 2)] += sib_in[1, pl.ds(0, 2)]
        start(row_back[1][:2])
        arrive(col_back[1])
        col_grad[1, 3] += col_in[1, 0] + col_in[1, 1]
        pair_back.start()

    events = {
        1: before1,
        3: before3,
        5: before5,
        7: before7,
        8: before8,
        9: before9,
        10: before10,
        12: before12,
    }

    score(0, 0)

    def pair(i, carry):
        for u in range(2):
            for s, event in events.items():
                if s % 2 == u:
                    pl.when(i == s // 2)(event)
            work(2 * i + u, u)
        return carry

    lax.fori_loop(0, 7, pair, 0)
    before14()
    work(14, 0)
    before15()
    work(15, 1, ahead=False)

    sib_back[2].start()
    sib_back[2].wait_recv()
    row_grad[q, 1, pl.ds(2, 2)] += sib_in[1, pl.ds(2, 2)]
    row_back[1][2].start()
    far_back.wait_recv()
    col_grad[0, 2] += col_in[1, 2]
    col_back[0][2].start()
    arrive(row_back[1])
    row_grad[q, 1, 3] += (row_in[1, 0] + row_in[1, 1]) + row_in[1, 2]
    feed[1].start()
    for s in range(2):
        slot = row_feed.at[s]
        pltpu.make_async_copy(slot, slot, recv_sems.at[feed_sem + s]).wait()
    row_feed[0] += row_feed[1]

    @pl.when(jnp.logical_not(ends_here))
    def _():
        home.start()

    arrive(col_back[0])
    col_grad[0, 3] += (col_in[0, 0] + col_in[0, 1]) + col_in[0, 2]
    pair_back.wait_recv()
    grad_ref[...] = (col_grad[0, 3] + col_last[...]).T

    @pl.when(is_owner)
    def _():
        for k in range(2):
            part = pl.ds(k * half, half)

            @pl.when(x_place[k] == x)
            def _():
                grad_ref[part, :] += row_feed[0]

            @pl.when(x_place[k] != x)
            def _():
                slot = row_home.at[k]
                pltpu.make_async_copy(slot, slot, recv_sems.at[home_sem + k]).wait()
                grad_ref[part, :] += row_home[k]

        for copy in scatter:
            copy.wait_send()

    @pl.when(jnp.logical_not(relay_self))
    def _():
        feed[0].wait_send()

    feed[1].wait_send()

    @pl.when(jnp.logical_not(ends_here))
    def _():
        home.wait_send()

    net.finish()


def local(cooc, tile_list, marginal, embed, accum):
    share, width = embed.shape
    half = share // 2
    items = 8 * share
    f32, bf16 = jnp.float32, jnp.bfloat16
    hbm = pl.BlockSpec(memory_space=pl.ANY)
    vmem = pl.BlockSpec(memory_space=pltpu.VMEM)
    summed = pl.pallas_call(
        kernel,
        out_shape=jax.ShapeDtypeStruct((share, width), f32),
        in_specs=[hbm, hbm, hbm, hbm],
        out_specs=vmem,
        scratch_shapes=[
            pltpu.VMEM((2, 4, share + PAD, width), f32),
            pltpu.VMEM((2, 2, 4, half + PAD, width), f32),
            pltpu.VMEM((2, half + PAD, width), f32),
            pltpu.VMEM((items, items), jnp.int32),
            pltpu.VMEM((items, width), bf16),
            pltpu.VMEM((items, width), bf16),
            pltpu.VMEM((8, width, share), bf16),
            pltpu.VMEM((8, width, share), bf16),
            pltpu.VMEM((items, width), bf16),
            pltpu.VMEM((items, width), bf16),
            pltpu.VMEM((items, 128), f32),
            pltpu.VMEM((8, PAD, share), f32),
            pltpu.VMEM((2, 2 * share, 2 * share), f32),
            pltpu.VMEM((2, 2, 4, half, width), f32),
            pltpu.VMEM((2, 4, width, share), f32),
            pltpu.VMEM((2, 4, half, width), f32),
            pltpu.VMEM((2, 3, half, width), f32),
            pltpu.VMEM((2, half, width), f32),
            pltpu.VMEM((2, half, width), f32),
            pltpu.VMEM((2, 3, width, share), f32),
            pltpu.VMEM((width, share), f32),
            pltpu.VMEM((1, share), jnp.int32),
            pltpu.SMEM((1, 4), jnp.int32),
            pltpu.VMEM((8, 8, 128), f32),
            pltpu.VMEM((4, 8, 128), f32),
            pltpu.VMEM((4, 8, 128), f32),
            pltpu.SemaphoreType.DMA((N_SEND,)),
            pltpu.SemaphoreType.DMA((N_RECV,)),
            pltpu.SemaphoreType.DMA((11,)),
        ],
        compiler_params=pltpu.CompilerParams(
            collective_id=0, has_side_effects=True, vmem_limit_bytes=56 * 2**20
        ),
        cost_estimate=pl.CostEstimate(
            flops=18 * items * items * width, bytes_accessed=4 * items * items, transcendentals=0
        ),
    )(embed, marginal.reshape(1, share), tile_list.reshape(1, 4), cooc)
    gradients = summed / (items // 2)
    new_accum = accum + gradients * gradients
    new_embed = embed - LEARN_RATE * gradients / jnp.sqrt(new_accum)
    return (new_embed, new_accum)


def solution(mesh):
    placed = (
        P("row", "col"),
        P("row", "col", None),
        P(("col", "row")),
        P(("col", "row"), None),
        P(("col", "row"), None),
    )
    return jax.shard_map(
        local,
        mesh=mesh,
        in_specs=placed,
        out_specs=(P(("col", "row"), None), P(("col", "row"), None)),
        check_vma=False,
    )
```
